256 devices in a mesh: expert: 16 (over y_hi, z), hidden: 16 (over x, y_lo, core).
Axes of the slice: x: 4, y: 4 (y_hi: 2, y_lo: 2; y = y_hi * 2 + y_lo), z: 8, core: 2. Of those that a mesh axis runs over, the one named last changes fastest.
Arguments:
- tokens: bfloat16 [16384, 2048], P(('expert', 'hidden')), may hold values from -6 to 6
- cotangent: bfloat16 [16384, 2048], P(('expert', 'hidden')), may hold values from -6 to 6
- order: int32 [256, 64], P(('expert', 'hidden')), may hold values from 0 to 63, each once within a row
- w_in: bfloat16 [16, 2048, 8192], P('expert', None, 'hidden'), may hold values from -0.125 to 0.125
- w_out: bfloat16 [16, 8192, 2048], P('expert', 'hidden'), may hold values from -0.0625 to 0.0625
- gains: float32 [16, 2048], P('expert'), may hold values from 0.5 to 1.5
- centroids: float32 [16, 2048], P('expert'), may hold values from -0.125 to 0.125
- saved_pre: bfloat16 [16, 1024, 8192], P('expert', None, 'hidden'), may hold values from -6 to 6
- saved_out: bfloat16 [16, 1024, 2048], P('expert', 'hidden'), may hold values from -6 to 6
Outputs:
- grad_tokens: bfloat16 [16384, 2048], P(('expert', 'hidden'))
- grad_w_in: bfloat16 [16, 2048, 8192], P('expert', None, 'hidden')
- grad_w_out: bfloat16 [16, 8192, 2048], P('expert', 'hidden')
- grad_gains: float32 [16, 2048], P('expert')
- grad_centroids: float32 [16, 2048], P('expert')
The draws below stay inside these ranges and needn't reach their ends.
Inputs may be any that keep to these rules, and one draw needn't show every extreme that they name: Each row of order is a permutation of 0 to 63, so each device assigns exactly 4 rows to each expert.
All inputs are finite; a program needn't handle non-finite values.
Results may differ from the reference program's by a relative error of at most 0.023.
Values may be sent and summed in bfloat16 or wider, within the bound.
A program may use at most 128 MiB of HBM per device.

```python
import jax
import jax.numpy as jnp
from jax import lax

D = 2048
FF = 8192
TOK_DEV = 64
EXPERTS = 16
SLOTS = 4
EXP_ROWS = 1024
TOKENS = 16384
N_EXPERT = 16
N_HIDDEN = 16
DEVICES = 256


def shard_levels(own_key, dims, split, least, top_value):
    gain = 1.0
    for axis_at, shards_of in split:
        draws = jax.random.uniform(jax.random.fold_in(jax.random.fold_in(own_key, 6), axis_at), (shards_of,), jnp.float32, least / len(split), top_value / len(split))
        gain = gain * jnp.repeat(jnp.exp(draws), dims[axis_at] // shards_of).reshape((-1,) + (1,) * (len(dims) - 1 - axis_at))
    return gain


def scatter_about(own_key, shape, scale, limit, split=(), kind=jnp.bfloat16):
    drawn = scale * jax.random.normal(own_key, shape, jnp.float32)
    if split:
        drawn = drawn * shard_levels(own_key, shape, split, -0.22, 0.18)
    return jnp.clip(drawn, -limit, limit).astype(kind)


def setup_inputs(seed: int = 0) -> dict:
    keys = jax.random.split(jax.random.key(seed), 10)
    return {
        "tokens": scatter_about(keys[0], (TOKENS, D), 1.0, 6.0, ((0, 256),)),
        "cotangent": scatter_about(keys[1], (TOKENS, D), 1.0, 6.0, ((0, 256),)),
        "order": jax.vmap(lambda own: jax.random.permutation(own, TOK_DEV))(jax.random.split(keys[2], DEVICES)).reshape((DEVICES, TOK_DEV)).astype(jnp.int32),
        "w_in": scatter_about(keys[3], (EXPERTS, D, FF), D ** -0.5, 0.125, ((0, 16), (2, 16))),
        "w_out": scatter_about(keys[4], (EXPERTS, FF, D), FF ** -0.5, 0.0625, ((0, 16), (1, 16))),
        "gains": jnp.clip(0.5 + 1.0 * jax.random.uniform(keys[5], (EXPERTS, D), jnp.float32) ** shard_levels(keys[5], (EXPERTS, D), ((0, 16),), -0.2, 0.2), 0.5, 1.5),
        "centroids": scatter_about(keys[6], (EXPERTS, D), D ** -0.5, 0.125, ((0, 16),), jnp.float32),
        "saved_pre": scatter_about(keys[7], (EXPERTS, EXP_ROWS, FF), 1.0, 6.0, ((0, 16), (2, 16))),
        "saved_out": scatter_about(keys[8], (EXPERTS, EXP_ROWS, D), 1.0, 6.0, ((0, 16), (1, 16))),
    }


def gelu_pair(value):
    result, pull = jax.vjp(lambda u: jax.nn.gelu(u, approximate=True), value)
    return (result, pull(jnp.ones_like(value))[0])

def expert_grads(args):
    x, dy, w_first, w_second, norm_gain, expert_centroid, pre, zout = args
    input_flat = x.astype(jnp.float32)
    output_gradient_flat = dy.astype(jnp.float32)
    reciprocal_norm = lax.rsqrt(lax.optimization_barrier(jnp.mean(input_flat * input_flat, axis=-1, keepdims=True)) + 1e-06)
    normalized_input = input_flat * reciprocal_norm
    normalized_rows = (normalized_input * norm_gain).astype(jnp.bfloat16)
    gate_weight = jax.nn.sigmoid(lax.optimization_barrier(jnp.sum(input_flat * expert_centroid, axis=-1)))
    dgate = lax.optimization_barrier(jnp.sum(output_gradient_flat * (input_flat + zout.astype(jnp.float32)), axis=-1))
    logit_gradient = dgate * gate_weight * (1.0 - gate_weight)
    output_gradient_gated = (gate_weight[:, None] * output_gradient_flat).astype(jnp.bfloat16)
    act, slope = gelu_pair(pre.astype(jnp.float32))
    act = act.astype(jnp.bfloat16)
    d_act = jnp.dot(output_gradient_gated, w_second.T, preferred_element_type=jnp.float32)
    d_pre = (d_act * slope).astype(jnp.bfloat16)
    g_first = jnp.dot(normalized_rows.T, d_pre, preferred_element_type=jnp.float32).astype(jnp.bfloat16)
    g_second = jnp.dot(act.T, output_gradient_gated, preferred_element_type=jnp.float32).astype(jnp.bfloat16)
    norm_gradient = jnp.dot(d_pre, w_first.T, preferred_element_type=jnp.float32)
    gain_gradient = lax.optimization_barrier(jnp.sum(norm_gradient * normalized_input, axis=0))
    g_cent = lax.optimization_barrier(jnp.sum(logit_gradient[:, None] * input_flat, axis=0))
    scaled_rows = norm_gradient * norm_gain
    input_gradient = output_gradient_flat * (1.0 + gate_weight[:, None]) + reciprocal_norm * (scaled_rows - normalized_input * lax.optimization_barrier(jnp.mean(scaled_rows * normalized_input, axis=-1, keepdims=True))) + logit_gradient[:, None] * expert_centroid
    return (input_gradient.astype(jnp.bfloat16), g_first, g_second, gain_gradient, g_cent)

def to_experts(rows, order4):
    slots = jnp.take_along_axis(rows, order4[..., None], axis=2)
    slots = slots.reshape(N_EXPERT, N_HIDDEN, N_EXPERT, SLOTS, D)
    return slots.transpose(2, 1, 0, 3, 4).reshape(EXPERTS, EXP_ROWS, D)

def reference(tokens, cotangent, order, w_in, w_out, gains, centroids, saved_pre, saved_out):
    order4 = order.reshape(N_EXPERT, N_HIDDEN, TOK_DEV).astype(jnp.int32)
    xe = to_experts(tokens.reshape(N_EXPERT, N_HIDDEN, TOK_DEV, D), order4)
    dye = to_experts(cotangent.reshape(N_EXPERT, N_HIDDEN, TOK_DEV, D), order4)
    input_gradient, g_first, g_second, gain_gradient, g_cent = lax.map(expert_grads, (xe, dye, w_in, w_out, gains, centroids, saved_pre, saved_out))
    back = input_gradient.reshape(N_EXPERT, N_HIDDEN, N_EXPERT, SLOTS, D).transpose(2, 1, 0, 3, 4)
    back = back.reshape(N_EXPERT, N_HIDDEN, TOK_DEV, D)
    inverse = jnp.argsort(order4, axis=-1).astype(jnp.int32)
    grad_tokens = jnp.take_along_axis(back, inverse[..., None], axis=2).reshape(TOKENS, D)
    return (grad_tokens, g_first, g_second, gain_gradient, g_cent)
```

```python
import functools

import jax
import jax.numpy as jnp
from jax import lax
from jax.experimental import pallas as pl
from jax.experimental.pallas import tpu as pltpu
from jax.sharding import PartitionSpec as P

MESH = pl.DeviceIdType.MESH
F32 = jnp.float32
BF16 = jnp.bfloat16
N = 16
ROWS = 64
D = 2048
FD = 512
CH = 512
HALF = 32


def dot_nn(a, b):
    return jnp.dot(a, b, preferred_element_type=F32)


def dot_nt(a, b):
    return lax.dot_general(a, b, (((1,), (1,)), ((), ())), preferred_element_type=F32)


def dot_tn(a, b):
    return lax.dot_general(a, b, (((0,), (0,)), ((), ())), preferred_element_type=F32)


def iota(shape, dim):
    return lax.broadcasted_iota(jnp.int32, shape, dim)


def onehot(mask):
    return jnp.where(mask, 1.0, 0.0).astype(BF16)


def chunk_pick(c, rows_first):
    shape = (ROWS, 256) if rows_first else (256, ROWS)
    k = iota(shape, 0 if rows_first else 1)
    q = iota(shape, 1 if rows_first else 0)
    return onehot(q == ((k >> 2) << 4) + 4 * c + (k & 3))


def gelu_pair(v):
    k0, k1 = 0.7978845608028654, 0.044715
    v2 = v * v
    t = jnp.tanh(k0 * (v + k1 * v2 * v))
    a = 0.5 * v * (1.0 + t)
    g = 0.5 * (1.0 + t) + 0.5 * v * (1.0 - t * t) * (k0 * (1.0 + 3.0 * k1 * v2))
    return a, g


def kernel(
    tok, cot, order, win_h, wout_h, gains, cent, pre_h, zout_h,
    gt_o, gwi_o, gwo_o, gg_o, gc_o,
    win, wout, pre, zout, act, slope, dh, dh2,
    a_dy, a_x, r_dy, r_x, dy, x, part, rc, fa, fb, fc, fr1, fr2, stat, vec, dxs, rb, stage_i, stage_o,
    load_sem, a2a_s, a2a_r, stat_s, stat_r, vec_s, vec_r, ret_s, ret_r, ag_s, ag_r, rs_s, rs_r, out_sem,
):
    e = lax.axis_index("expert")
    h = lax.axis_index("hidden")
    xi = h // 4
    yc = h % 4
    yi = yc // 2
    ci = yc % 2
    yo = 1 - yi
    co = 1 - ci
    yoc = 2 * yo + ci
    xp, xm = (h + 4) % N, (h + 12) % N
    yn = h + 2 * (yo - yi)
    cn = h + co - ci

    barrier = pltpu.get_barrier_semaphore()

    @pl.loop(1, N)
    def _(i):
        pl.semaphore_signal(barrier, 1, device_id={"expert": (e + i) % N, "hidden": h}, device_id_type=MESH)
        pl.semaphore_signal(barrier, 1, device_id={"expert": e, "hidden": (h + i) % N}, device_id_type=MESH)

    loads = [
        pltpu.make_async_copy(pre_h.at[0, pl.ds(pl.multiple_of(((xi + k) % 4) * 256, 256), 256)], pre.at[k], load_sem.at[k])
        for k in range(4)
    ]
    loads.append(pltpu.make_async_copy(zout_h.at[0], zout, load_sem.at[4]))
    loads.append(pltpu.make_async_copy(wout_h.at[0], wout, load_sem.at[5]))
    loads.append(pltpu.make_async_copy(win_h.at[0], win, load_sem.at[6]))
    for c in loads:
        c.start()

    to_slot = onehot(iota((ROWS, ROWS), 0) == order[...])
    q = iota((256, ROWS), 0)
    spread = onehot(iota((256, ROWS), 1) == ((q >> 4) << 2) + (q & 3))
    pick = dot_nt(spread, to_slot)
    chunk_of = (q >> 2) & 3
    picks = [jnp.where(chunk_of == c, pick, 0.0).astype(BF16) for c in range(4)]

    def dispatch(src, dst):
        acc = dot_nn(picks[0], src[:, 0:CH])
        for c in range(1, 4):
            acc += dot_nn(picks[c], src[:, c * CH : (c + 1) * CH])
        dst[...] = acc.astype(BF16).reshape(N, 16, CH)

    def a2a_copy(src, dst, ssem, rsem, i):
        return pltpu.make_async_remote_copy(
            src_ref=src.at[(e + i) % N], dst_ref=dst.at[e], send_sem=ssem, recv_sem=rsem,
            device_id={"expert": (e + i) % N, "hidden": h}, device_id_type=MESH,
        )

    def a2a_start(t, src, dst):
        @pl.loop(1, N)
        def _(i):
            a2a_copy(src, dst, a2a_s.at[t, i], a2a_r.at[t, i], i).start()

        dst[e] = src[e]

    def a2a_arrived(t, src, dst):
        @pl.loop(1, N)
        def _(i):
            pltpu.make_async_remote_copy(
                src_ref=src.at[(e + i) % N], dst_ref=dst.at[(e + N - i) % N], send_sem=a2a_s.at[t, i], recv_sem=a2a_r.at[t, i],
                device_id={"expert": (e + i) % N, "hidden": h}, device_id_type=MESH,
            ).wait()

    dispatch(cot, a_dy)
    pl.semaphore_wait(barrier, 2 * (N - 1))
    a2a_start(0, a_dy, r_dy)
    dispatch(tok, a_x)
    a2a_start(1, a_x, r_x)

    for k in range(4):
        loads[k].wait()

    @pl.loop(0, 16)
    def _(i):
        k, rows = i // 4, pl.ds(pl.multiple_of((i % 4) * 64, 64), 64)
        a, g = gelu_pair(pre[k, rows].astype(F32))
        act[k, rows] = a.astype(BF16)
        slope[k, rows] = g

    def remote(sems, i, src, dst, where):
        return pltpu.make_async_remote_copy(
            src_ref=src, dst_ref=dst, send_sem=sems[0].at[i], recv_sem=sems[1].at[i],
            device_id={"expert": e, "hidden": where}, device_id_type=MESH,
        )

    def gather_plan(t, buf):
        sems = (ag_s.at[t], ag_r.at[t])
        lo, hi = pl.ds(0, HALF), pl.ds(HALF, HALF)
        plan = {
            "own_xp": (buf.at[0, yc], buf.at[3, yc], xp, buf.at[3, yc]),
            "own_xm": (buf.at[0, yc], buf.at[1, yc], xm, buf.at[1, yc]),
            "own_y": (buf.at[0, yc], buf.at[0, yc], yn, buf.at[0, yoc]),
            "half_xp": (buf.at[3, yc, lo], buf.at[2, yc, lo], xp, buf.at[2, yc, lo]),
            "half_xm": (buf.at[1, yc, hi], buf.at[2, yc, hi], xm, buf.at[2, yc, hi]),
            "oy_xp": (buf.at[0, yoc], buf.at[3, yoc], xp, buf.at[3, yoc]),
            "oy_xm": (buf.at[0, yoc], buf.at[1, yoc], xm, buf.at[1, yoc]),
            "far_y": (buf.at[2, yc], buf.at[2, yc], yn, buf.at[2, yoc]),
        }
        for k in range(4):
            plan["core_%d" % k] = (buf.at[k, yc], buf.at[k, yc], cn, buf.at[k, 2 * yi + co])
            plan["core_y%d" % k] = (buf.at[k, yoc], buf.at[k, yoc], cn, buf.at[k, 2 * yo + co])
        out = {}
        for i, (name, (src, dst, where, got)) in enumerate(plan.items()):
            out[name] = (remote(sems, i, src, dst, where), remote(sems, i, src, got, where))
        return out

    class Gather:
        def __init__(self, t, buf):
            self.plan = gather_plan(t, buf)

        def start(self, *names):
            for n in names:
                self.plan[n][0].start()

        def got(self, *names):
            for n in names:
                self.plan[n][1].wait_recv()

        def sent(self, *names):
            for n in names:
                self.plan[n][0].wait_send()

        def sent_all(self):
            self.sent(*self.plan)

    def collect(src, dst):
        rows = src[...].reshape(256, CH)
        for c in range(4):
            dst[0, yc, :, c * CH : (c + 1) * CH] = dot_nn(chunk_pick(c, True), rows).astype(BF16)

    gd = Gather(0, dy)
    gx = Gather(1, x)

    a2a_arrived(0, a_dy, r_dy)
    collect(r_dy, dy)
    gd.start("own_xp", "own_xm", "own_y", "core_0")

    a2a_arrived(1, a_x, r_x)
    collect(r_x, x)

    loads[4].wait()
    xf = x[0, yc].astype(F32)
    dyf = dy[0, yc].astype(F32)
    r = lax.rsqrt(jnp.sum(xf * xf, axis=1, keepdims=True) * (1.0 / D) + 1e-06)
    s = jax.nn.sigmoid(jnp.sum(xf * cent[...], axis=1, keepdims=True))
    ds = jnp.sum(dyf * (xf + zout[...].astype(F32)), axis=1, keepdims=True)
    dlogit = ds * s * (1.0 - s)
    row_i, lane_i = iota((ROWS, 128), 0), iota((ROWS, 128), 1)
    s_mask, r_mask = lane_i == row_i, lane_i == row_i + ROWS
    stat[0, yc] = jnp.sum(jnp.where(s_mask, s, 0.0) + jnp.where(r_mask, r, 0.0), axis=0, keepdims=True)
    vec[h, 1:2] = jnp.sum(dlogit * xf, axis=0, keepdims=True)

    def stat_copy(i, got):
        to, frm = (h + i) % N, (h + N - i) % N
        slot = ((frm // 4 + 4 - xi) % 4, frm % 4) if got else ((xi + 4 - to // 4) % 4, yc)
        return pltpu.make_async_remote_copy(
            src_ref=stat.at[0, yc], dst_ref=stat.at[slot[0], slot[1]], send_sem=stat_s.at[i], recv_sem=stat_r.at[i],
            device_id={"expert": e, "hidden": to}, device_id_type=MESH,
        )

    @pl.loop(1, N)
    def _(i):
        stat_copy(i, False).start()

    gd.got("own_xp", "own_xm", "own_y")
    gd.start("half_xp", "half_xm", "oy_xp", "oy_xm", "core_1", "core_3", "core_y0")

    @pl.loop(1, N)
    def _(i):
        stat_copy(i, True).wait()

    loads[5].wait()
    loads[6].wait()

    def forward(k):
        acc = [dot_nt(dy[k].reshape(256, D), wout[f * 256 : (f + 1) * 256]) for f in range(2)]
        for j in range(4):
            rows = slice(j * ROWS, (j + 1) * ROWS)
            line = stat[k, j]
            sj = jnp.sum(jnp.where(s_mask, line, 0.0), axis=1, keepdims=True)
            rj = jnp.sum(jnp.where(r_mask, line, 0.0), axis=1, keepdims=True)
            for f in range(2):
                cols = slice(f * 256, (f + 1) * 256)
                v = acc[f][rows] * (slope[k, rows, cols] * sj)
                dh[k, rows, cols] = v.astype(BF16)
                dh2[k, rows, cols] = (v * rj).astype(BF16)
                act[k, rows, cols] = (act[k, rows, cols].astype(F32) * sj).astype(BF16)

        @pl.loop(0, 8)
        def _(n):
            cols = pl.ds(pl.multiple_of(n * 256, 256), 256)
            t = dot_nt(dh[k], win[cols]).astype(BF16)
            for j in range(4):
                part[j % 2, k, j // 2, :, cols] = t[j * ROWS : (j + 1) * ROWS]

    rs_sems = (rs_s, rs_r)
    core_rs = [remote(rs_sems, k, part.at[co, k], rc.at[k], cn) for k in range(4)]

    gd.got("core_0", "core_y0")
    forward(0)
    core_rs[0].start()
    gd.got("half_xp", "half_xm")
    gd.start("far_y", "core_2")
    gd.got("oy_xp", "oy_xm")
    gd.start("core_y1", "core_y3")
    gd.got("far_y")
    gd.start("core_y2")
    gx.start("own_xp", "own_xm", "own_y", "core_0")
    gd.got("core_1", "core_y1")
    forward(1)
    core_rs[1].start()
    gd.got("core_3", "core_y3")
    forward(3)
    core_rs[3].start()
    gd.got("core_2", "core_y2")
    forward(2)
    core_rs[2].start()

    def add(dst, *others):
        total = dst[...].astype(F32)
        for o in others:
            total += o[...].astype(F32)
        dst[...] = total.astype(BF16)

    def both_cores(k):
        core_rs[k].wait_recv()
        add(part.at[ci, k], rc.at[k])

    rs = {
        "a_p": remote(rs_sems, 4, part.at[ci, 1, yo], fa.at[0], xp),
        "a_m": remote(rs_sems, 5, part.at[ci, 3, yo], fa.at[1], xm),
        "r1": remote(rs_sems, 6, part.at[ci, 2, yo], fr1, yn),
        "b_p": remote(rs_sems, 7, part.at[ci, 2, yi, pl.ds(0, HALF)], fb.at[0], xp),
        "b_m": remote(rs_sems, 8, part.at[ci, 2, yi, pl.ds(HALF, HALF)], fb.at[1], xm),
        "r2": remote(rs_sems, 9, part.at[ci, 0, yo], fr2, yn),
        "c_p": remote(rs_sems, 10, part.at[ci, 1, yi], fc.at[0], xp),
        "c_m": remote(rs_sems, 11, part.at[ci, 3, yi], fc.at[1], xm),
    }
    both_cores(1)
    rs["a_p"].start()
    both_cores(3)
    rs["a_m"].start()
    both_cores(2)
    rs["r1"].start()
    both_cores(0)
    gx.got("own_xp", "own_xm", "own_y")
    gx.start("half_xp", "half_xm", "core_1", "core_3", "core_y0")

    out_copies = []

    def weight_out(n):
        cols = slice(n * 512, (n + 1) * 512)
        stage_o[:, cols] = dot_tn(
            act[...].reshape(N * ROWS, FD), dy[:, :, :, cols].reshape(N * ROWS, 512)
        ).astype(BF16)

    for n in range(4):
        weight_out(n)
    out_copies.append(pltpu.make_async_copy(stage_o, gwo_o.at[0], out_sem.at[0]))
    out_copies[-1].start()

    rs["r1"].wait_recv()
    add(part.at[ci, 2, yi], fr1)
    rs["b_p"].start()
    rs["b_m"].start()
    rs["a_p"].wait_recv()
    rs["a_m"].wait_recv()
    add(part.at[ci, 0, yo], fa.at[0], fa.at[1])
    rs["r2"].start()
    rs["b_p"].wait_recv()
    add(part.at[ci, 1, yi, pl.ds(0, HALF)], fb.at[0])
    rs["c_p"].start()
    rs["b_m"].wait_recv()
    add(part.at[ci, 3, yi, pl.ds(HALF, HALF)], fb.at[1])
    rs["c_m"].start()
    gx.start("oy_xp", "oy_xm")
    gx.got("half_xp", "half_xm")
    gx.start("far_y", "core_2")

    rs["r2"].wait_recv()
    rs["c_p"].wait_recv()
    rs["c_m"].wait_recv()
    dn = (
        part[ci, 0, yi].astype(F32) + fr2[...].astype(F32) + fc[0].astype(F32) + fc[1].astype(F32)
    )
    xf = x[0, yc].astype(F32)
    dyf = dy[0, yc].astype(F32)
    xhat = xf * r
    vec[h, 0:1] = jnp.sum(dn * xhat, axis=0, keepdims=True)
    qv = dn * gains[...]
    m = jnp.sum(qv * xhat, axis=1, keepdims=True) * (1.0 / D)
    dx = (dyf * (1.0 + s) + r * (qv - xhat * m) + dlogit * cent[...]).astype(BF16)
    acc = dot_nn(chunk_pick(0, False), dx[:, 0:CH])
    for c in range(1, 4):
        acc += dot_nn(chunk_pick(c, False), dx[:, c * CH : (c + 1) * CH])
    dxs[...] = acc.astype(BF16).reshape(N, 16, CH)

    def ret_copy(i, got):
        return pltpu.make_async_remote_copy(
            src_ref=dxs.at[(e + i) % N], dst_ref=rb.at[(e + N - i) % N if got else e],
            send_sem=ret_s.at[i], recv_sem=ret_r.at[i],
            device_id={"expert": (e + i) % N, "hidden": h}, device_id_type=MESH,
        )

    def vec_copy(i, got):
        return pltpu.make_async_remote_copy(
            src_ref=vec.at[h], dst_ref=vec.at[(h + N - i) % N if got else h], send_sem=vec_s.at[i], recv_sem=vec_r.at[i],
            device_id={"expert": e, "hidden": (h + i) % N}, device_id_type=MESH,
        )

    @pl.loop(1, N)
    def _(i):
        ret_copy(i, False).start()

    @pl.loop(1, N)
    def _(i):
        vec_copy(i, False).start()

    rb[e] = dxs[e]

    gx.got("oy_xp", "oy_xm")
    gx.start("core_y1", "core_y3")
    gx.got("far_y")
    gx.start("core_y2")
    gx.got(*["core_%d" % k for k in range(4)], *["core_y%d" % k for k in range(4)])

    eye = iota((256, 256), 0) == iota((256, 256), 1)
    for n in range(8):
        cols = slice(n * 256, (n + 1) * 256)
        gain = jnp.sum(jnp.where(eye, gains[:, cols], 0.0), axis=1, keepdims=True)
        t = dot_tn(x[:, :, :, cols].reshape(N * ROWS, 256), dh2[...].reshape(N * ROWS, FD))
        stage_i[cols] = (t * gain).astype(BF16)
    out_copies.append(pltpu.make_async_copy(stage_i, gwi_o.at[0], out_sem.at[1]))
    out_copies[-1].start()

    @pl.loop(1, N)
    def _(i):
        ret_copy(i, True).wait()
        vec_copy(i, True).wait()

    back = rb[...].reshape(256, CH)
    slot_of = dot_nt(to_slot, spread)
    q2 = iota((ROWS, 256), 1)
    for c in range(4):
        w = jnp.where(((q2 >> 2) & 3) == c, slot_of, 0.0).astype(BF16)
        gt_o[:, c * CH : (c + 1) * CH] = dot_nn(w, back).astype(BF16)
    total = vec[0]
    for i in range(1, N):
        total += vec[i]
    gg_o[...] = total[0:1]
    gc_o[...] = total[1:2]

    gd.sent_all()
    gx.sent_all()
    for c in core_rs:
        c.wait_send()
    for c in rs.values():
        c.wait_send()
    for c in out_copies:
        c.wait()


def shards(*args):
    vm = pl.BlockSpec(memory_space=pltpu.VMEM)
    hbm = pl.BlockSpec(memory_space=pl.ANY)
    rows4 = (4, 4, ROWS, D)
    dma = pltpu.SemaphoreType.DMA
    return pl.pallas_call(
        kernel,
        out_shape=(
            jax.ShapeDtypeStruct((ROWS, D), BF16),
            jax.ShapeDtypeStruct((1, D, FD), BF16),
            jax.ShapeDtypeStruct((1, FD, D), BF16),
            jax.ShapeDtypeStruct((1, D), F32),
            jax.ShapeDtypeStruct((1, D), F32),
        ),
        in_specs=[vm, vm, vm, hbm, hbm, vm, vm, hbm, hbm],
        out_specs=(vm, hbm, hbm, vm, vm),
        scratch_shapes=[
            pltpu.VMEM((D, FD), BF16),
            pltpu.VMEM((FD, D), BF16),
            pltpu.VMEM((4, 256, FD), BF16),
            pltpu.VMEM((ROWS, D), BF16),
            pltpu.VMEM((4, 256, FD), BF16),
            pltpu.VMEM((4, 256, FD), F32),
            pltpu.VMEM((4, 256, FD), BF16),
            pltpu.VMEM((4, 256, FD), BF16),
            pltpu.VMEM((N, 16, CH), BF16),
            pltpu.VMEM((N, 16, CH), BF16),
            pltpu.VMEM((N, 16, CH), BF16),
            pltpu.VMEM((N, 16, CH), BF16),
            pltpu.VMEM(rows4, BF16),
            pltpu.VMEM(rows4, BF16),
            pltpu.VMEM((2, 4, 2, ROWS, D), BF16),
            pltpu.VMEM((4, 2, ROWS, D), BF16),
            pltpu.VMEM((2, ROWS, D), BF16),
            pltpu.VMEM((2, HALF, D), BF16),
            pltpu.VMEM((2, ROWS, D), BF16),
            pltpu.VMEM((ROWS, D), BF16),
            pltpu.VMEM((ROWS, D), BF16),
            pltpu.VMEM((4, 4, 1, 128), F32),
            pltpu.VMEM((N, 2, D), F32),
            pltpu.VMEM((N, 16, CH), BF16),
            pltpu.VMEM((N, 16, CH), BF16),
            pltpu.VMEM((D, FD), BF16),
            pltpu.VMEM((FD, D), BF16),
            dma((7,)),
            dma((2, N)), dma((2, N)),
            dma((N,)), dma((N,)),
            dma((N,)), dma((N,)),
            dma((N,)), dma((N,)),
            dma((2, 16)), dma((2, 16)),
            dma((12,)), dma((12,)),
            dma((2,)),
        ],
        compiler_params=pltpu.CompilerParams(
            collective_id=0, has_side_effects=True, vmem_limit_bytes=56 * 2**20
        ),
    )(*args)


def solution(mesh):
    placed = (
        P(("expert", "hidden"), None),
        P(("expert", "hidden"), None),
        P(("expert", "hidden"), None),
        P("expert", None, "hidden"),
        P("expert", "hidden", None),
        P("expert", None),
        P("expert", None),
        P("expert", None, "hidden"),
        P("expert", "hidden", None),
    )
    return jax.shard_map(
        shards,
        mesh=mesh,
        in_specs=placed,
        out_specs=(
            P(("expert", "hidden"), None),
            P("expert", None, "hidden"),
            P("expert", "hidden", None),
            P("expert", None),
            P("expert", None),
        ),
        check_vma=False,
    )
```

```python
import functools

import jax
import jax.numpy as jnp
from jax import lax
from jax.experimental import pallas as pl
from jax.experimental.pallas import tpu as pltpu
from jax.sharding import PartitionSpec as P

MESH = pl.DeviceIdType.MESH
F32 = jnp.float32
BF16 = jnp.bfloat16
N = 16
ROWS = 64
D = 2048
FD = 512
CH = 512
HALF = 32
VMEM_BYTES = 44 * 2**20


def dot_nn(a, b):
    return jnp.dot(a, b, preferred_element_type=F32)


def dot_nt(a, b):
    return lax.dot_general(a, b, (((1,), (1,)), ((), ())), preferred_element_type=F32)


def dot_tn(a, b):
    return lax.dot_general(a, b, (((0,), (0,)), ((), ())), preferred_element_type=F32)


def iota(shape, dim):
    return lax.broadcasted_iota(jnp.int32, shape, dim)


def onehot(mask):
    return jnp.where(mask, 1.0, 0.0).astype(BF16)


def chunk_pick(c, rows_first):
    shape = (ROWS, 256) if rows_first else (256, ROWS)
    k = iota(shape, 0 if rows_first else 1)
    q = iota(shape, 1 if rows_first else 0)
    return onehot(q == ((k >> 2) << 4) + 4 * c + (k & 3))


def gelu_pair(v):
    k0, k1 = 0.7978845608028654, 0.044715
    v2 = v * v
    t = jnp.tanh(k0 * (v + k1 * v2 * v))
    a = 0.5 * v * (1.0 + t)
    g = 0.5 * (1.0 + t) + 0.5 * v * (1.0 - t * t) * (k0 * (1.0 + 3.0 * k1 * v2))
    return a, g


def kernel(
    tok, cot, order, win_h, wout_h, gains, cent, pre_h, zout_h,
    gt_o, gwi_o, gwo_o, vec_o,
    win_t, wout_t, pre, zout, act, slope, dh,
    a_dy, a_x, r_dy, r_x, dy, x, part, rc, fa, fb, fc, fr1, fr2, stat, vec, dxs, rb,
    load_sem, a2a_s, a2a_r, stat_s, stat_r, vec_s, vec_r, ret_s, ret_r, ag_s, ag_r, rs_s, rs_r,
):
    e = lax.axis_index("expert")
    h = lax.axis_index("hidden")
    xi = h // 4
    yc = h % 4
    yi = yc // 2
    ci = yc % 2
    yo = 1 - yi
    co = 1 - ci
    yoc = 2 * yo + ci
    xp, xm = (h + 4) % N, (h + 12) % N
    yn = h + 2 * (yo - yi)
    cn = h + co - ci

    barrier = pltpu.get_barrier_semaphore()

    @pl.loop(1, N)
    def _(i):
        pl.semaphore_signal(barrier, 1, device_id={"expert": (e + i) % N, "hidden": h}, device_id_type=MESH)
        pl.semaphore_signal(barrier, 1, device_id={"expert": e, "hidden": (h + i) % N}, device_id_type=MESH)

    loads = [
        pltpu.make_async_copy(pre_h.at[0, pl.ds(pl.multiple_of(((xi + k) % 4) * 256, 256), 256)], pre.at[k], load_sem.at[k])
        for k in range(4)
    ]
    loads.append(pltpu.make_async_copy(zout_h.at[0], zout, load_sem.at[4]))
    loads.append(pltpu.make_async_copy(wout_h.at[0], gwo_o, load_sem.at[5]))
    loads.append(pltpu.make_async_copy(win_h.at[0], gwi_o, load_sem.at[6]))
    for c in loads:
        c.start()

    to_slot = onehot(iota((ROWS, ROWS), 0) == order[...])
    q = iota((256, ROWS), 0)
    spread = onehot(iota((256, ROWS), 1) == ((q >> 4) << 2) + (q & 3))
    pick = dot_nt(spread, to_slot)
    chunk_of = (q >> 2) & 3
    picks = [jnp.where(chunk_of == c, pick, 0.0).astype(BF16) for c in range(4)]

    def dispatch(src, dst):
        acc = dot_nn(picks[0], src[:, 0:CH])
        for c in range(1, 4):
            acc += dot_nn(picks[c], src[:, c * CH : (c + 1) * CH])
        dst[...] = acc.astype(BF16).reshape(N, 16, CH)

    def a2a_copy(src, dst, ssem, rsem, i):
        return pltpu.make_async_remote_copy(
            src_ref=src.at[(e + i) % N], dst_ref=dst.at[e], send_sem=ssem, recv_sem=rsem,
            device_id={"expert": (e + i) % N, "hidden": h}, device_id_type=MESH,
        )

    def a2a_start(t, src, dst):
        @pl.loop(1, N)
        def _(i):
            a2a_copy(src, dst, a2a_s.at[t, i], a2a_r.at[t, i], i).start()

        dst[e] = src[e]

    def a2a_arrived(t, src, dst):
        @pl.loop(1, N)
        def _(i):
            pltpu.make_async_remote_copy(
                src_ref=src.at[(e + i) % N], dst_ref=dst.at[(e + N - i) % N], send_sem=a2a_s.at[t, i], recv_sem=a2a_r.at[t, i],
                device_id={"expert": (e + i) % N, "hidden": h}, device_id_type=MESH,
            ).wait()

    dispatch(cot, a_dy)
    pl.semaphore_wait(barrier, 2 * (N - 1))
    a2a_start(0, a_dy, r_dy)
    dispatch(tok, a_x)
    a2a_start(1, a_x, r_x)

    loads[5].wait()
    wout_t[...] = gwo_o[...].T
    loads[6].wait()
    win_t[...] = gwi_o[...].T

    for k in range(4):
        loads[k].wait()

    @pl.loop(0, 16)
    def _(i):
        k, rows = i // 4, pl.ds(pl.multiple_of((i % 4) * 64, 64), 64)
        a, g = gelu_pair(pre[k, rows].astype(F32))
        act[k, rows] = a.astype(BF16)
        slope[k, rows] = g

    lo, hi = pl.ds(0, HALF), pl.ds(HALF, HALF)

    def remote(sems, i, src, dst, where):
        return pltpu.make_async_remote_copy(
            src_ref=src, dst_ref=dst, send_sem=sems[0].at[i], recv_sem=sems[1].at[i],
            device_id={"expert": e, "hidden": where}, device_id_type=MESH,
        )

    def gather_plan(t, buf):
        sems = (ag_s.at[t], ag_r.at[t])
        plan = {}
        for part_of, r in (("lo", lo), ("hi", hi)):
            plan["own_xp_" + part_of] = (buf.at[0, yc, r], buf.at[3, yc, r], xp, buf.at[3, yc, r])
            plan["own_xm_" + part_of] = (buf.at[0, yc, r], buf.at[1, yc, r], xm, buf.at[1, yc, r])
            plan["own_y_" + part_of] = (buf.at[0, yc, r], buf.at[0, yc, r], yn, buf.at[0, yoc, r])
            plan["oy_xp_" + part_of] = (buf.at[0, yoc, r], buf.at[3, yoc, r], xp, buf.at[3, yoc, r])
            plan["oy_xm_" + part_of] = (buf.at[0, yoc, r], buf.at[1, yoc, r], xm, buf.at[1, yoc, r])
            plan["far_y_" + part_of] = (buf.at[2, yc, r], buf.at[2, yc, r], yn, buf.at[2, yoc, r])
        plan["half_xp"] = (buf.at[3, yc, lo], buf.at[2, yc, lo], xp, buf.at[2, yc, lo])
        plan["half_xm"] = (buf.at[1, yc, hi], buf.at[2, yc, hi], xm, buf.at[2, yc, hi])
        for k in range(4):
            plan["core_%d" % k] = (buf.at[k, yc], buf.at[k, yc], cn, buf.at[k, 2 * yi + co])
            plan["core_y%d" % k] = (buf.at[k, yoc], buf.at[k, yoc], cn, buf.at[k, 2 * yo + co])
        out = {}
        for i, (name, (src, dst, where, got)) in enumerate(plan.items()):
            out[name] = (remote(sems, i, src, dst, where), remote(sems, i, src, got, where))
        return out

    class Gather:
        def __init__(self, t, buf):
            self.plan = gather_plan(t, buf)

        def start(self, *names):
            for n in names:
                self.plan[n][0].start()

        def got(self, *names):
            for n in names:
                self.plan[n][1].wait_recv()

        def sent(self, *names):
            for n in names:
                self.plan[n][0].wait_send()

        def sent_all(self):
            self.sent(*self.plan)

    def collect(src, dst):
        rows = src[...].reshape(256, CH)
        for c in range(4):
            dst[0, yc, :, c * CH : (c + 1) * CH] = dot_nn(chunk_pick(c, True), rows).astype(BF16)

    gd = Gather(0, dy)
    gx = Gather(1, x)

    def first_hop(g):
        g.start("own_xp_lo", "own_xm_hi", "own_y_lo", "own_xp_hi", "own_xm_lo", "own_y_hi", "core_0")

    def second_hop_a(g):
        g.got("own_xp_lo")
        g.start("half_xp")
        g.got("own_xm_hi")
        g.start("half_xm")

    def second_hop_b(g):
        g.got("own_y_lo")
        g.start("oy_xp_lo", "oy_xm_lo")
        g.got("own_y_hi")
        g.start("oy_xp_hi", "oy_xm_hi", "core_y0")
        g.got("own_xm_lo")
        g.start("core_1")
        g.got("own_xp_hi")
        g.start("core_3")

    def third_hop(g):
        g.got("half_xp")
        g.start("far_y_lo")
        g.got("half_xm")
        g.start("far_y_hi", "core_2")

    def last_hop(g):
        g.got("oy_xp_lo", "oy_xp_hi")
        g.start("core_y3")
        g.got("oy_xm_lo", "oy_xm_hi")
        g.start("core_y1")

    def last_far(g):
        g.got("far_y_lo", "far_y_hi")
        g.start("core_y2")

    def forward(k, y):
        rows = pl.ds(pl.multiple_of(y * 128, 128), 128)
        acc = dot_nn(dy[k, pl.ds(2 * y, 2)].reshape(128, D), wout_t[...])
        dh_rows = (acc * slope[k, rows]).astype(BF16)
        dh[k, rows] = dh_rows
        t = dot_nn(dh_rows, win_t[...]).astype(BF16)
        part[0, k, y] = t[:ROWS]
        part[1, k, y] = t[ROWS:]

    rs_sems = (rs_s, rs_r)
    core_rs = {}
    for k in range(4):
        core_rs[k, 0] = remote(rs_sems, 2 * k, part.at[co, k, yi], rc.at[k, yi], cn)
        core_rs[k, 1] = remote(rs_sems, 2 * k + 1, part.at[co, k, yo], rc.at[k, yo], cn)

    def forward_send(k, other):
        forward(k, yo if other else yi)
        core_rs[k, other].start()

    def add(dst, *others):
        total = dst[...].astype(F32)
        for o in others:
            total += o[...].astype(F32)
        dst[...] = total.astype(BF16)

    def both_cores(k, other):
        core_rs[k, other].wait_recv()
        y = yo if other else yi
        add(part.at[ci, k, y], rc.at[k, y])

    rs = {
        "b_p": remote(rs_sems, 8, part.at[ci, 2, yi, lo], fb.at[0], xp),
        "b_m": remote(rs_sems, 9, part.at[ci, 2, yi, hi], fb.at[1], xm),
        "c_p": remote(rs_sems, 10, part.at[ci, 1, yi, lo], fc.at[0, lo], xp),
        "c_m": remote(rs_sems, 11, part.at[ci, 3, yi, hi], fc.at[1, hi], xm),
        "free_p": remote(rs_sems, 12, part.at[ci, 1, yi, hi], fc.at[0, hi], xp),
        "free_m": remote(rs_sems, 13, part.at[ci, 3, yi, lo], fc.at[1, lo], xm),
    }
    for i, (part_of, r) in enumerate((("lo", lo), ("hi", hi))):
        rs["a_p_" + part_of] = remote(rs_sems, 14 + 4 * i, part.at[ci, 1, yo, r], fa.at[0, r], xp)
        rs["a_m_" + part_of] = remote(rs_sems, 15 + 4 * i, part.at[ci, 3, yo, r], fa.at[1, r], xm)
        rs["r1_" + part_of] = remote(rs_sems, 16 + 4 * i, part.at[ci, 2, yo, r], fr1.at[r], yn)
        rs["r2_" + part_of] = remote(rs_sems, 17 + 4 * i, part.at[ci, 0, yo, r], fr2.at[r], yn)

    a2a_arrived(0, a_dy, r_dy)
    collect(r_dy, dy)
    first_hop(gd)
    gd.got("core_0")
    forward_send(0, 0)
    second_hop_a(gd)
    second_hop_b(gd)
    gd.got("core_1")
    forward_send(1, 0)
    both_cores(0, 0)
    third_hop(gd)
    gd.got("core_3")
    forward_send(3, 0)
    both_cores(1, 0)
    rs["free_p"].start()

    a2a_arrived(1, a_x, r_x)
    collect(r_x, x)

    loads[4].wait()
    xf = x[0, yc].astype(F32)
    dyf = dy[0, yc].astype(F32)
    r = lax.rsqrt(jnp.sum(xf * xf, axis=1, keepdims=True) * (1.0 / D) + 1e-06)
    s = jax.nn.sigmoid(jnp.sum(xf * cent[...], axis=1, keepdims=True))
    ds = jnp.sum(dyf * (xf + zout[...].astype(F32)), axis=1, keepdims=True)
    dlogit = ds * s * (1.0 - s)
    row_i, lane_i = iota((ROWS, 128), 0), iota((ROWS, 128), 1)
    s_mask, r_mask = lane_i == row_i, lane_i == row_i + ROWS
    stat[0, yc] = jnp.sum(jnp.where(s_mask, s, 0.0) + jnp.where(r_mask, r, 0.0), axis=0, keepdims=True)
    vec[h, 1] = jnp.sum(dlogit * xf, axis=0, keepdims=True)

    def stat_copy(i, got):
        to, frm = (h + i) % N, (h + N - i) % N
        slot = ((frm // 4 + 4 - xi) % 4, frm % 4) if got else ((xi + 4 - to // 4) % 4, yc)
        return pltpu.make_async_remote_copy(
            src_ref=stat.at[0, yc], dst_ref=stat.at[slot[0], slot[1]], send_sem=stat_s.at[i], recv_sem=stat_r.at[i],
            device_id={"expert": e, "hidden": to}, device_id_type=MESH,
        )

    @pl.loop(1, N)
    def _(i):
        stat_copy(i, False).start()

    both_cores(3, 0)
    rs["free_m"].start()
    gd.got("core_y0")
    forward_send(0, 1)
    gd.got("core_2")
    forward_send(2, 0)
    last_hop(gd)
    first_hop(gx)
    last_far(gd)
    gd.got("core_y1")
    forward_send(1, 1)
    gd.got("core_y3")
    forward_send(3, 1)
    both_cores(1, 1)
    rs["a_p_lo"].start()
    rs["a_p_hi"].start()
    gd.got("core_y2")
    forward_send(2, 1)
    both_cores(3, 1)
    rs["a_m_lo"].start()
    rs["a_m_hi"].start()
    both_cores(2, 1)
    rs["r1_lo"].start()
    rs["r1_hi"].start()
    both_cores(2, 0)
    both_cores(0, 1)

    @pl.loop(1, N)
    def _(i):
        stat_copy(i, True).wait()

    @pl.loop(0, 16)
    def _(i):
        k, j = i // 4, i % 4
        rows = pl.ds(pl.multiple_of(j * ROWS, ROWS), ROWS)
        line = stat[k, j]
        sj = jnp.sum(jnp.where(s_mask, line, 0.0), axis=1, keepdims=True)
        rj = jnp.sum(jnp.where(r_mask, line, 0.0), axis=1, keepdims=True)
        act[k, rows] = (act[k, rows].astype(F32) * sj).astype(BF16)
        dh[k, rows] = (dh[k, rows].astype(F32) * (sj * rj)).astype(BF16)

    def weight_out(n):
        cols = slice(n * 1024, (n + 1) * 1024)
        gwo_o[:, cols] = dot_tn(
            act[...].reshape(N * ROWS, FD), dy[:, :, :, cols].reshape(N * ROWS, 1024)
        ).astype(BF16)

    rs["r1_lo"].wait_recv()
    add(part.at[ci, 2, yi, lo], fr1.at[lo])
    rs["b_p"].start()
    rs["r1_hi"].wait_recv()
    add(part.at[ci, 2, yi, hi], fr1.at[hi])
    rs["b_m"].start()
    second_hop_a(gx)
    for part_of, half in (("lo", lo), ("hi", hi)):
        rs["a_p_" + part_of].wait_recv()
        rs["a_m_" + part_of].wait_recv()
        add(part.at[ci, 0, yo, half], fa.at[0, half], fa.at[1, half])
        rs["r2_" + part_of].start()
    rs["b_p"].wait_recv()
    add(part.at[ci, 1, yi, lo], fb.at[0])
    rs["c_p"].start()
    rs["b_m"].wait_recv()
    add(part.at[ci, 3, yi, hi], fb.at[1])
    rs["c_m"].start()
    second_hop_b(gx)
    third_hop(gx)
    weight_out(0)
    weight_out(1)

    for n in ("r2_lo", "r2_hi", "c_p", "c_m", "free_p", "free_m"):
        rs[n].wait_recv()
    dn = s * (
        part[ci, 0, yi].astype(F32) + fr2[...].astype(F32) + fc[0].astype(F32) + fc[1].astype(F32)
    )
    xf = x[0, yc].astype(F32)
    dyf = dy[0, yc].astype(F32)
    xhat = xf * r
    vec[h, 0] = jnp.sum(dn * xhat, axis=0, keepdims=True)
    qv = dn * gains[...]
    m = jnp.sum(qv * xhat, axis=1, keepdims=True) * (1.0 / D)
    dx = (dyf * (1.0 + s) + r * (qv - xhat * m) + dlogit * cent[...]).astype(BF16)
    acc = dot_nn(chunk_pick(0, False), dx[:, 0:CH])
    for c in range(1, 4):
        acc += dot_nn(chunk_pick(c, False), dx[:, c * CH : (c + 1) * CH])
    dxs[...] = acc.astype(BF16).reshape(N, 16, CH)

    def ret_copy(i, got):
        return pltpu.make_async_remote_copy(
            src_ref=dxs.at[(e + i) % N], dst_ref=rb.at[(e + N - i) % N if got else e],
            send_sem=ret_s.at[i], recv_sem=ret_r.at[i],
            device_id={"expert": (e + i) % N, "hidden": h}, device_id_type=MESH,
        )

    def vec_copy(i, got):
        return pltpu.make_async_remote_copy(
            src_ref=vec.at[h], dst_ref=vec.at[(h + N - i) % N if got else h], send_sem=vec_s.at[i], recv_sem=vec_r.at[i],
            device_id={"expert": e, "hidden": (h + i) % N}, device_id_type=MESH,
        )

    @pl.loop(1, N)
    def _(i):
        ret_copy(i, False).start()

    @pl.loop(1, N)
    def _(i):
        vec_copy(i, False).start()

    rb[e] = dxs[e]

    last_hop(gx)
    last_far(gx)
    gx.got(*["core_%d" % k for k in range(4)], *["core_y%d" % k for k in range(4)])

    eye = iota((256, 256), 0) == iota((256, 256), 1)
    for n in range(8):
        cols = slice(n * 256, (n + 1) * 256)
        gain = jnp.sum(jnp.where(eye, gains[:, cols], 0.0), axis=1, keepdims=True)
        t = dot_tn(x[:, :, :, cols].reshape(N * ROWS, 256), dh[...].reshape(N * ROWS, FD))
        gwi_o[cols] = (t * gain).astype(BF16)

    @pl.loop(1, N)
    def _(i):
        ret_copy(i, True).wait()
        vec_copy(i, True).wait()

    back = rb[...].reshape(256, CH)
    slot_of = dot_nt(to_slot, spread)
    q2 = iota((ROWS, 256), 1)
    for c in range(4):
        w = jnp.where(((q2 >> 2) & 3) == c, slot_of, 0.0).astype(BF16)
        gt_o[:, c * CH : (c + 1) * CH] = dot_nn(w, back).astype(BF16)
    total = vec[0]
    for i in range(1, N):
        total += vec[i]
    vec_o[...] = total

    gd.sent_all()
    gx.sent_all()
    for c in (*core_rs.values(), *rs.values()):
        c.wait_send()


def write_out(gt, gwi, gwo, vec, gt_o, gwi_o, gwo_o, gg_o, gc_o, sem):
    pairs = ((gwi, gwi_o.at[0]), (gwo, gwo_o.at[0]), (gt, gt_o), (vec.at[0], gg_o), (vec.at[1], gc_o))
    copies = [pltpu.make_async_copy(a, b, sem.at[i]) for i, (a, b) in enumerate(pairs)]
    for c in copies:
        c.start()
    for c in copies:
        c.wait()


def shards(*args):
    vm = pl.BlockSpec(memory_space=pltpu.VMEM)
    hbm = pl.BlockSpec(memory_space=pltpu.HBM)
    anywhere = pl.BlockSpec(memory_space=pl.ANY)
    rows4 = (4, 4, ROWS, D)
    dma = pltpu.SemaphoreType.DMA
    args = [pltpu.with_memory_space_constraint(a, pltpu.HBM) for a in args]
    results = pl.pallas_call(
        kernel,
        out_shape=(
            pltpu.VMEM((ROWS, D), BF16),
            pltpu.VMEM((D, FD), BF16),
            pltpu.VMEM((FD, D), BF16),
            pltpu.VMEM((2, 1, D), F32),
        ),
        in_specs=[vm, vm, vm, hbm, hbm, vm, vm, hbm, hbm],
        out_specs=(vm,) * 4,
        scratch_shapes=[
            pltpu.VMEM((FD, D), BF16),
            pltpu.VMEM((D, FD), BF16),
            pltpu.VMEM((4, 256, FD), BF16),
            pltpu.VMEM((ROWS, D), BF16),
            pltpu.VMEM((4, 256, FD), BF16),
            pltpu.VMEM((4, 256, FD), F32),
            pltpu.VMEM((4, 256, FD), BF16),
            pltpu.VMEM((N, 16, CH), BF16),
            pltpu.VMEM((N, 16, CH), BF16),
            pltpu.VMEM((N, 16, CH), BF16),
            pltpu.VMEM((N, 16, CH), BF16),
            pltpu.VMEM(rows4, BF16),
            pltpu.VMEM(rows4, BF16),
            pltpu.VMEM((2, 4, 2, ROWS, D), BF16),
            pltpu.VMEM((4, 2, ROWS, D), BF16),
            pltpu.VMEM((2, ROWS, D), BF16),
            pltpu.VMEM((2, HALF, D), BF16),
            pltpu.VMEM((2, ROWS, D), BF16),
            pltpu.VMEM((ROWS, D), BF16),
            pltpu.VMEM((ROWS, D), BF16),
            pltpu.VMEM((4, 4, 1, 128), F32),
            pltpu.VMEM((N, 2, 1, D), F32),
            pltpu.VMEM((N, 16, CH), BF16),
            pltpu.VMEM((N, 16, CH), BF16),
            dma((7,)),
            dma((2, N)), dma((2, N)),
            dma((N,)), dma((N,)),
            dma((N,)), dma((N,)),
            dma((N,)), dma((N,)),
            dma((2, 22)), dma((2, 22)),
            dma((22,)), dma((22,)),
        ],
        compiler_params=pltpu.CompilerParams(
            collective_id=0, has_side_effects=True, vmem_limit_bytes=VMEM_BYTES
        ),
    )(*args)
    return pl.pallas_call(
        write_out,
        out_shape=(
            jax.ShapeDtypeStruct((ROWS, D), BF16),
            jax.ShapeDtypeStruct((1, D, FD), BF16),
            jax.ShapeDtypeStruct((1, FD, D), BF16),
            jax.ShapeDtypeStruct((1, D), F32),
            jax.ShapeDtypeStruct((1, D), F32),
        ),
        in_specs=[anywhere] * 4,
        out_specs=(hbm,) * 5,
        scratch_shapes=[dma((5,))],
        compiler_params=pltpu.CompilerParams(vmem_limit_bytes=2**20),
    )(*results)


def solution(mesh):
    placed = (
        P(("expert", "hidden"), None),
        P(("expert", "hidden"), None),
        P(("expert", "hidden"), None),
        P("expert", None, "hidden"),
        P("expert", "hidden", None),
        P("expert", None),
        P("expert", None),
        P("expert", None, "hidden"),
        P("expert", "hidden", None),
    )
    return jax.shard_map(
        shards,
        mesh=mesh,
        in_specs=placed,
        out_specs=(
            P(("expert", "hidden"), None),
            P("expert", None, "hidden"),
            P("expert", "hidden", None),
            P("expert", None),
            P("expert", None),
        ),
        check_vma=False,
    )
```

```python
import functools

import jax
import jax.numpy as jnp
from jax import lax
from jax.experimental import pallas as pl
from jax.experimental.pallas import tpu as pltpu
from jax.sharding import PartitionSpec as P

MESH = pl.DeviceIdType.MESH
F32 = jnp.float32
BF16 = jnp.bfloat16
N = 16
ROWS = 64
D = 2048
FD = 512
CH = 512
HALF = 32
VMEM_BYTES = 44 * 2**20


def dot_nn(a, b):
    return jnp.dot(a, b, preferred_element_type=F32)


def dot_nt(a, b):
    return lax.dot_general(a, b, (((1,), (1,)), ((), ())), preferred_element_type=F32)


def dot_tn(a, b):
    return lax.dot_general(a, b, (((0,), (0,)), ((), ())), preferred_element_type=F32)


def iota(shape, dim):
    return lax.broadcasted_iota(jnp.int32, shape, dim)


def onehot(mask):
    return jnp.where(mask, 1.0, 0.0).astype(BF16)


def chunk_pick(c, rows_first):
    shape = (ROWS, 256) if rows_first else (256, ROWS)
    k = iota(shape, 0 if rows_first else 1)
    q = iota(shape, 1 if rows_first else 0)
    return onehot(q == ((k >> 2) << 4) + 4 * c + (k & 3))


def gelu_pair(v):
    k0, k1 = 0.7978845608028654, 0.044715
    v2 = v * v
    t = jnp.tanh(k0 * (v + k1 * v2 * v))
    a = 0.5 * v * (1.0 + t)
    g = 0.5 * (1.0 + t) + 0.5 * v * (1.0 - t * t) * (k0 * (1.0 + 3.0 * k1 * v2))
    return a, g


def kernel(
    tok_h, cot_h, order_h, win_h, wout_h, gains_h, cent_h, pre_h, zout_h,
    gt_o, gwi_o, gwo_o, vec_o,
    tok, cot, order, gains, cent, win_t, wout_t, pre, pre_s, zout, act, slope, slope_s, dh, dh_s,
    a_dy, a_x, r_dy, r_x, dy, x, part, fa, fb, fc, fr1, fr2, stat, vec, dxs, rb,
    load_sem, a2a_s, a2a_r, stat_s, stat_r, vec_s, vec_r, ret_s, ret_r, ag_s, ag_r, rs_s, rs_r, pair_s, pair_r,
):
    e = lax.axis_index("expert")
    h = lax.axis_index("hidden")
    xi = h // 4
    yc = h % 4
    yi = yc // 2
    ci = yc % 2
    yo = 1 - yi
    co = 1 - ci
    yoc = 2 * yo + ci
    xp, xm = (h + 4) % N, (h + 12) % N
    yn = h + 2 * (yo - yi)
    cn = h + co - ci

    barrier = pltpu.get_barrier_semaphore()

    @pl.loop(1, N)
    def _(i):
        pl.semaphore_signal(barrier, 1, device_id={"expert": (e + i) % N, "hidden": h}, device_id_type=MESH)
        pl.semaphore_signal(barrier, 1, device_id={"expert": e, "hidden": (h + i) % N}, device_id_type=MESH)

    sources = [(order_h, order), (cot_h, cot), (tok_h, tok), (wout_h.at[0], gwo_o), (win_h.at[0], gwi_o)]
    sources += [(pre_h.at[0, pl.ds(pl.multiple_of(((xi + k) % 4) * 256, 256), 256)], pre.at[k]) for k in range(4)]
    sources += [(cent_h, cent), (gains_h, gains), (zout_h.at[0], zout)]
    loads = [pltpu.make_async_copy(src, dst, load_sem.at[i]) for i, (src, dst) in enumerate(sources)]
    for c in loads:
        c.start()

    loads[0].wait()
    to_slot = onehot(iota((ROWS, ROWS), 0) == order[...])
    q = iota((256, ROWS), 0)
    spread = onehot(iota((256, ROWS), 1) == ((q >> 4) << 2) + (q & 3))
    pick = dot_nt(spread, to_slot)
    chunk_of = (q >> 2) & 3
    picks = [jnp.where(chunk_of == c, pick, 0.0).astype(BF16) for c in range(4)]

    def dispatch(src, dst):
        acc = dot_nn(picks[0], src[:, 0:CH])
        for c in range(1, 4):
            acc += dot_nn(picks[c], src[:, c * CH : (c + 1) * CH])
        dst[...] = acc.astype(BF16).reshape(N, 16, CH)

    def a2a_copy(src, dst, ssem, rsem, i):
        return pltpu.make_async_remote_copy(
            src_ref=src.at[(e + i) % N], dst_ref=dst.at[e], send_sem=ssem, recv_sem=rsem,
            device_id={"expert": (e + i) % N, "hidden": h}, device_id_type=MESH,
        )

    def a2a_start(t, src, dst):
        @pl.loop(1, N)
        def _(i):
            a2a_copy(src, dst, a2a_s.at[t, i], a2a_r.at[t, i], i).start()

        dst[e] = src[e]

    def a2a_arrived(t, src, dst):
        @pl.loop(1, N)
        def _(i):
            pltpu.make_async_remote_copy(
                src_ref=src.at[(e + i) % N], dst_ref=dst.at[(e + N - i) % N], send_sem=a2a_s.at[t, i], recv_sem=a2a_r.at[t, i],
                device_id={"expert": (e + i) % N, "hidden": h}, device_id_type=MESH,
            ).wait()

    loads[1].wait()
    dispatch(cot, a_dy)
    pl.semaphore_wait(barrier, 2 * (N - 1))
    a2a_start(0, a_dy, r_dy)
    loads[2].wait()
    dispatch(tok, a_x)
    a2a_start(1, a_x, r_x)

    lo, hi = pl.ds(0, HALF), pl.ds(HALF, HALF)

    def remote(sems, i, src, dst, where):
        return pltpu.make_async_remote_copy(
            src_ref=src, dst_ref=dst, send_sem=sems[0].at[i], recv_sem=sems[1].at[i],
            device_id={"expert": e, "hidden": where}, device_id_type=MESH,
        )

    pair_sems = (pair_s, pair_r)
    blocks = [(k, y) for k in range(4) for y in range(2)]

    def rows_of(y, c):
        return pl.ds(pl.multiple_of((2 * y + c) * ROWS, ROWS), ROWS)

    pair = [remote(pair_sems, i, pre.at[k, rows_of(y, co)], pre_s.at[k, y], cn) for i, (k, y) in enumerate(blocks)]
    pair.append(remote(pair_sems, 8, wout_t.at[0], wout_t.at[1], cn))
    pair.append(remote(pair_sems, 9, win_t.at[0], win_t.at[1], cn))
    loads[3].wait()
    wout_t[0] = gwo_o[...].T
    pair[8].start()
    for k in range(4):
        loads[5 + k].wait()
    for c in pair[:8]:
        c.start()
    loads[4].wait()
    win_t[0] = gwi_o[...].T
    pair[9].start()

    @pl.loop(0, 16)
    def _(i):
        k, rows = i // 4, pl.ds(pl.multiple_of((i % 4) * ROWS, ROWS), ROWS)
        a, g = gelu_pair(pre[k, rows].astype(F32))
        act[k, rows] = a.astype(BF16)
        slope[k, rows] = g

    def gather_plan(t, buf):
        sems = (ag_s.at[t], ag_r.at[t])
        plan = {}
        for part_of, r in (("lo", lo), ("hi", hi)):
            plan["own_xp_" + part_of] = (buf.at[0, yc, r], buf.at[3, yc, r], xp, buf.at[3, yc, r])
            plan["own_xm_" + part_of] = (buf.at[0, yc, r], buf.at[1, yc, r], xm, buf.at[1, yc, r])
            plan["own_y_" + part_of] = (buf.at[0, yc, r], buf.at[0, yc, r], yn, buf.at[0, yoc, r])
            plan["oy_xp_" + part_of] = (buf.at[0, yoc, r], buf.at[3, yoc, r], xp, buf.at[3, yoc, r])
            plan["oy_xm_" + part_of] = (buf.at[0, yoc, r], buf.at[1, yoc, r], xm, buf.at[1, yoc, r])
            plan["far_y_" + part_of] = (buf.at[2, yc, r], buf.at[2, yc, r], yn, buf.at[2, yoc, r])
        plan["half_xp"] = (buf.at[3, yc, lo], buf.at[2, yc, lo], xp, buf.at[2, yc, lo])
        plan["half_xm"] = (buf.at[1, yc, hi], buf.at[2, yc, hi], xm, buf.at[2, yc, hi])
        for k in range(4):
            plan["core_%d" % k] = (buf.at[k, yc], buf.at[k, yc], cn, buf.at[k, 2 * yi + co])
            plan["core_y%d" % k] = (buf.at[k, yoc], buf.at[k, yoc], cn, buf.at[k, 2 * yo + co])
        out = {}
        for i, (name, (src, dst, where, got)) in enumerate(plan.items()):
            out[name] = (remote(sems, i, src, dst, where), remote(sems, i, src, got, where))
        return out

    class Gather:
        def __init__(self, t, buf):
            self.plan = gather_plan(t, buf)

        def start(self, *names):
            for n in names:
                self.plan[n][0].start()

        def got(self, *names):
            for n in names:
                self.plan[n][1].wait_recv()

        def sent(self, *names):
            for n in names:
                self.plan[n][0].wait_send()

        def sent_all(self):
            self.sent(*self.plan)

    def collect(src, dst):
        rows = src[...].reshape(256, CH)
        for c in range(4):
            dst[0, yc, :, c * CH : (c + 1) * CH] = dot_nn(chunk_pick(c, True), rows).astype(BF16)

    gd = Gather(0, dy)
    gx = Gather(1, x)

    def first_hop_x(g):
        g.start("own_xp_lo", "own_xm_hi", "own_xp_hi", "own_xm_lo", "core_0")

    def first_hop_y(g):
        g.start("own_y_lo", "own_y_hi")

    def second_hop_a(g):
        g.got("own_xp_lo")
        g.start("half_xp")
        g.got("own_xm_hi")
        g.start("half_xm")

    def second_hop_b(g):
        g.got("own_y_lo")
        g.start("oy_xp_lo", "oy_xm_lo")
        g.got("own_y_hi")
        g.start("oy_xp_hi", "oy_xm_hi", "core_y0")

    def first_cores(g):
        g.got("own_xm_lo")
        g.start("core_1")
        g.got("own_xp_hi")
        g.start("core_3")

    def third_hop(g):
        g.got("half_xp")
        g.start("far_y_lo")
        g.got("half_xm")
        g.start("far_y_hi", "core_2")

    def last_hop(g):
        g.got("oy_xp_lo", "oy_xp_hi")
        g.start("core_y3")
        g.got("oy_xm_lo", "oy_xm_hi")
        g.start("core_y1")

    def last_far(g):
        g.got("far_y_lo", "far_y_hi")
        g.start("core_y2")

    rs_sems = (rs_s, rs_r)
    dh_copies = {}
    for k in range(4):
        for other, y in ((0, yi), (1, yo)):
            dh_copies[k, other] = remote(rs_sems, 2 * k + other, dh_s.at[k, y], dh.at[k, rows_of(y, ci)], cn)

    def forward(*shares):
        at = [(k, yo if other else yi) for k, other in shares]
        rows = [dy[k, 2 * y + ci] for k, y in at]
        rows = jnp.concatenate(rows, axis=0) if len(rows) > 1 else rows[0]
        mine, others = dot_nn(rows, wout_t[0]), dot_nn(rows, wout_t[1])
        left, right = [], []
        for i, (k, y) in enumerate(at):
            cut = slice(i * ROWS, (i + 1) * ROWS)
            left.append((mine[cut] * slope[k, rows_of(y, ci)]).astype(BF16))
            right.append((others[cut] * slope_s[k, y]).astype(BF16))
            dh[k, rows_of(y, ci)] = left[-1]
            dh_s[k, y] = right[-1]
        left = jnp.concatenate(left, axis=0) if len(at) > 1 else left[0]
        right = jnp.concatenate(right, axis=0) if len(at) > 1 else right[0]
        t = (dot_nn(left, win_t[0]) + dot_nn(right, win_t[1])).astype(BF16)
        for i, (k, y) in enumerate(at):
            part[k, y] = t[i * ROWS : (i + 1) * ROWS]
        for share in shares:
            dh_copies[share].start()

    def add(dst, *others):
        total = dst[...].astype(F32)
        for o in others:
            total += o[...].astype(F32)
        dst[...] = total.astype(BF16)

    rs = {
        "b_p": remote(rs_sems, 8, part.at[2, yi, lo], fb.at[0], xp),
        "b_m": remote(rs_sems, 9, part.at[2, yi, hi], fb.at[1], xm),
        "c_p": remote(rs_sems, 10, part.at[1, yi, lo], fc.at[0, lo], xp),
        "c_m": remote(rs_sems, 11, part.at[3, yi, hi], fc.at[1, hi], xm),
        "free_p": remote(rs_sems, 12, part.at[1, yi, hi], fc.at[0, hi], xp),
        "free_m": remote(rs_sems, 13, part.at[3, yi, lo], fc.at[1, lo], xm),
    }
    for i, (part_of, r) in enumerate((("lo", lo), ("hi", hi))):
        rs["a_p_" + part_of] = remote(rs_sems, 14 + 4 * i, part.at[1, yo, r], fa.at[0, r], xp)
        rs["a_m_" + part_of] = remote(rs_sems, 15 + 4 * i, part.at[3, yo, r], fa.at[1, r], xm)
        rs["r1_" + part_of] = remote(rs_sems, 16 + 4 * i, part.at[2, yo, r], fr1.at[r], yn)
        rs["r2_" + part_of] = remote(rs_sems, 17 + 4 * i, part.at[0, yo, r], fr2.at[r], yn)

    a2a_arrived(0, a_dy, r_dy)
    collect(r_dy, dy)
    first_hop_x(gd)
    first_hop_y(gd)
    for c in pair:
        c.wait_recv()

    @pl.loop(0, 8)
    def _(i):
        slope_s[i // 2, i % 2] = gelu_pair(pre_s[i // 2, i % 2].astype(F32))[1]

    second_hop_a(gd)
    second_hop_b(gd)
    a2a_arrived(1, a_x, r_x)
    collect(r_x, x)
    first_hop_x(gx)
    first_cores(gd)
    forward((1, 0), (3, 0), (0, 0), (0, 1))
    rs["free_p"].start()
    rs["free_m"].start()
    third_hop(gd)
    first_hop_y(gx)

    for c in loads[9:]:
        c.wait()
    xf = x[0, yc].astype(F32)
    dyf = dy[0, yc].astype(F32)
    r = lax.rsqrt(jnp.sum(xf * xf, axis=1, keepdims=True) * (1.0 / D) + 1e-06)
    s = jax.nn.sigmoid(jnp.sum(xf * cent[...], axis=1, keepdims=True))
    ds = jnp.sum(dyf * (xf + zout[...].astype(F32)), axis=1, keepdims=True)
    dlogit = ds * s * (1.0 - s)
    row_i, lane_i = iota((ROWS, 128), 0), iota((ROWS, 128), 1)
    s_mask, r_mask = lane_i == row_i, lane_i == row_i + ROWS
    stat[0, yc] = jnp.sum(jnp.where(s_mask, s, 0.0) + jnp.where(r_mask, r, 0.0), axis=0, keepdims=True)
    vec[h, 1] = jnp.sum(dlogit * xf, axis=0, keepdims=True)

    def stat_copy(i, got):
        to, frm = (h + i) % N, (h + N - i) % N
        slot = ((frm // 4 + 4 - xi) % 4, frm % 4) if got else ((xi + 4 - to // 4) % 4, yc)
        return pltpu.make_async_remote_copy(
            src_ref=stat.at[0, yc], dst_ref=stat.at[slot[0], slot[1]], send_sem=stat_s.at[i], recv_sem=stat_r.at[i],
            device_id={"expert": e, "hidden": to}, device_id_type=MESH,
        )

    @pl.loop(1, N)
    def _(i):
        stat_copy(i, False).start()

    forward((2, 0),)
    last_hop(gd)
    forward((1, 1), (3, 1))
    second_hop_a(gx)
    rs["a_p_lo"].start()
    rs["a_m_lo"].start()
    rs["a_p_hi"].start()
    rs["a_m_hi"].start()
    last_far(gd)
    forward((2, 1),)
    rs["r1_lo"].start()
    rs["r1_hi"].start()
    gd.got(*["core_%d" % k for k in range(4)], *["core_y%d" % k for k in range(4)])
    for c in dh_copies.values():
        c.wait_recv()

    @pl.loop(1, N)
    def _(i):
        stat_copy(i, True).wait()

    @pl.loop(0, 16)
    def _(i):
        k, j = i // 4, i % 4
        rows = pl.ds(pl.multiple_of(j * ROWS, ROWS), ROWS)
        line = stat[k, j]
        sj = jnp.sum(jnp.where(s_mask, line, 0.0), axis=1, keepdims=True)
        rj = jnp.sum(jnp.where(r_mask, line, 0.0), axis=1, keepdims=True)
        act[k, rows] = (act[k, rows].astype(F32) * sj).astype(BF16)
        dh[k, rows] = (dh[k, rows].astype(F32) * (sj * rj)).astype(BF16)

    def weight_out(n):
        cols = slice(n * 1024, (n + 1) * 1024)
        gwo_o[:, cols] = dot_tn(
            act[...].reshape(N * ROWS, FD), dy[:, :, :, cols].reshape(N * ROWS, 1024)
        ).astype(BF16)

    rs["r1_lo"].wait_recv()
    add(part.at[2, yi, lo], fr1.at[lo])
    rs["b_p"].start()
    rs["r1_hi"].wait_recv()
    add(part.at[2, yi, hi], fr1.at[hi])
    rs["b_m"].start()
    gx.got("own_y_lo")
    gx.start("oy_xp_lo", "oy_xm_lo")
    first_cores(gx)
    for part_of, half in (("lo", lo), ("hi", hi)):
        rs["a_p_" + part_of].wait_recv()
        rs["a_m_" + part_of].wait_recv()
        add(part.at[0, yo, half], fa.at[0, half], fa.at[1, half])
        rs["r2_" + part_of].start()
    rs["b_p"].wait_recv()
    add(part.at[1, yi, lo], fb.at[0])
    rs["c_p"].start()
    rs["b_m"].wait_recv()
    add(part.at[3, yi, hi], fb.at[1])
    rs["c_m"].start()
    gx.got("own_y_hi")
    gx.start("oy_xp_hi", "oy_xm_hi", "core_y0")
    third_hop(gx)
    weight_out(0)
    weight_out(1)

    for n in ("r2_lo", "r2_hi", "c_p", "c_m", "free_p", "free_m"):
        rs[n].wait_recv()
    dn = s * (
        part[0, yi].astype(F32) + fr2[...].astype(F32) + fc[0].astype(F32) + fc[1].astype(F32)
    )
    xf = x[0, yc].astype(F32)
    dyf = dy[0, yc].astype(F32)
    xhat = xf * r
    vec[h, 0] = jnp.sum(dn * xhat, axis=0, keepdims=True)
    qv = dn * gains[...]
    m = jnp.sum(qv * xhat, axis=1, keepdims=True) * (1.0 / D)
    dx = (dyf * (1.0 + s) + r * (qv - xhat * m) + dlogit * cent[...]).astype(BF16)
    acc = dot_nn(chunk_pick(0, False), dx[:, 0:CH])
    for c in range(1, 4):
        acc += dot_nn(chunk_pick(c, False), dx[:, c * CH : (c + 1) * CH])
    dxs[...] = acc.astype(BF16).reshape(N, 16, CH)

    def ret_copy(i, got):
        return pltpu.make_async_remote_copy(
            src_ref=dxs.at[(e + i) % N], dst_ref=rb.at[(e + N - i) % N if got else e],
            send_sem=ret_s.at[i], recv_sem=ret_r.at[i],
            device_id={"expert": (e + i) % N, "hidden": h}, device_id_type=MESH,
        )

    def vec_copy(i, got):
        return pltpu.make_async_remote_copy(
            src_ref=vec.at[h], dst_ref=vec.at[(h + N - i) % N if got else h], send_sem=vec_s.at[i], recv_sem=vec_r.at[i],
            device_id={"expert": e, "hidden": (h + i) % N}, device_id_type=MESH,
        )

    @pl.loop(1, N)
    def _(i):
        ret_copy(i, False).start()

    @pl.loop(1, N)
    def _(i):
        vec_copy(i, False).start()

    rb[e] = dxs[e]

    last_hop(gx)
    last_far(gx)
    gx.got(*["core_%d" % k for k in range(4)], *["core_y%d" % k for k in range(4)])

    eye = iota((256, 256), 0) == iota((256, 256), 1)
    for n in range(8):
        cols = slice(n * 256, (n + 1) * 256)
        gain = jnp.sum(jnp.where(eye, gains[:, cols], 0.0), axis=1, keepdims=True)
        t = dot_tn(x[:, :, :, cols].reshape(N * ROWS, 256), dh[...].reshape(N * ROWS, FD))
        gwi_o[cols] = (t * gain).astype(BF16)

    @pl.loop(1, N)
    def _(i):
        vec_copy(i, True).wait()

    total = vec[0]
    for i in range(1, N):
        total += vec[i]
    vec_o[...] = total

    @pl.loop(1, N)
    def _(i):
        ret_copy(i, True).wait()

    back = rb[...].reshape(256, CH)
    slot_of = dot_nt(to_slot, spread)
    q2 = iota((ROWS, 256), 1)
    for c in range(4):
        w = jnp.where(((q2 >> 2) & 3) == c, slot_of, 0.0).astype(BF16)
        gt_o[:, c * CH : (c + 1) * CH] = dot_nn(w, back).astype(BF16)

    gd.sent_all()
    gx.sent_all()
    for c in (*pair, *dh_copies.values(), *rs.values()):
        c.wait_send()


def write_out(gt, gwi, gwo, vec, gt_o, gwi_o, gwo_o, gg_o, gc_o, sem):
    pairs = ((gwi, gwi_o.at[0]), (gwo, gwo_o.at[0]), (gt, gt_o), (vec.at[0], gg_o), (vec.at[1], gc_o))
    copies = [pltpu.make_async_copy(a, b, sem.at[i]) for i, (a, b) in enumerate(pairs)]
    for c in copies:
        c.start()
    for c in copies:
        c.wait()


def shards(*args):
    vm = pl.BlockSpec(memory_space=pltpu.VMEM)
    hbm = pl.BlockSpec(memory_space=pltpu.HBM)
    anywhere = pl.BlockSpec(memory_space=pl.ANY)
    rows4 = (4, 4, ROWS, D)
    dma = pltpu.SemaphoreType.DMA
    args = [pltpu.with_memory_space_constraint(a, pltpu.HBM) for a in args]
    results = pl.pallas_call(
        kernel,
        out_shape=(
            pltpu.VMEM((ROWS, D), BF16),
            pltpu.VMEM((D, FD), BF16),
            pltpu.VMEM((FD, D), BF16),
            pltpu.VMEM((2, 1, D), F32),
        ),
        in_specs=[hbm] * 9,
        out_specs=(vm,) * 4,
        scratch_shapes=[
            pltpu.VMEM((ROWS, D), BF16),
            pltpu.VMEM((ROWS, D), BF16),
            pltpu.VMEM((1, ROWS), jnp.int32),
            pltpu.VMEM((1, D), F32),
            pltpu.VMEM((1, D), F32),
            pltpu.VMEM((2, FD, D), BF16),
            pltpu.VMEM((2, D, FD), BF16),
            pltpu.VMEM((4, 256, FD), BF16),
            pltpu.VMEM((4, 2, ROWS, FD), BF16),
            pltpu.VMEM((ROWS, D), BF16),
            pltpu.VMEM((4, 256, FD), BF16),
            pltpu.VMEM((4, 256, FD), F32),
            pltpu.VMEM((4, 2, ROWS, FD), F32),
            pltpu.VMEM((4, 256, FD), BF16),
            pltpu.VMEM((4, 2, ROWS, FD), BF16),
            pltpu.VMEM((N, 16, CH), BF16),
            pltpu.VMEM((N, 16, CH), BF16),
            pltpu.VMEM((N, 16, CH), BF16),
            pltpu.VMEM((N, 16, CH), BF16),
            pltpu.VMEM(rows4, BF16),
            pltpu.VMEM(rows4, BF16),
            pltpu.VMEM((4, 2, ROWS, D), BF16),
            pltpu.VMEM((2, ROWS, D), BF16),
            pltpu.VMEM((2, HALF, D), BF16),
            pltpu.VMEM((2, ROWS, D), BF16),
            pltpu.VMEM((ROWS, D), BF16),
            pltpu.VMEM((ROWS, D), BF16),
            pltpu.VMEM((4, 4, 1, 128), F32),
            pltpu.VMEM((N, 2, 1, D), F32),
            pltpu.VMEM((N, 16, CH), BF16),
            pltpu.VMEM((N, 16, CH), BF16),
            dma((12,)),
            dma((2, N)), dma((2, N)),
            dma((N,)), dma((N,)),
            dma((N,)), dma((N,)),
            dma((N,)), dma((N,)),
            dma((2, 22)), dma((2, 22)),
            dma((22,)), dma((22,)),
            dma((10,)), dma((10,)),
        ],
        compiler_params=pltpu.CompilerParams(
            collective_id=0, has_side_effects=True, vmem_limit_bytes=VMEM_BYTES
        ),
    )(*args)
    return pl.pallas_call(
        write_out,
        out_shape=(
            jax.ShapeDtypeStruct((ROWS, D), BF16),
            jax.ShapeDtypeStruct((1, D, FD), BF16),
            jax.ShapeDtypeStruct((1, FD, D), BF16),
            jax.ShapeDtypeStruct((1, D), F32),
            jax.ShapeDtypeStruct((1, D), F32),
        ),
        in_specs=[anywhere] * 4,
        out_specs=(hbm,) * 5,
        scratch_shapes=[dma((5,))],
        compiler_params=pltpu.CompilerParams(vmem_limit_bytes=2**20),
    )(*results)


def solution(mesh):
    placed = (
        P(("expert", "hidden"), None),
        P(("expert", "hidden"), None),
        P(("expert", "hidden"), None),
        P("expert", None, "hidden"),
        P("expert", "hidden", None),
        P("expert", None),
        P("expert", None),
        P("expert", None, "hidden"),
        P("expert", "hidden", None),
    )
    return jax.shard_map(
        shards,
        mesh=mesh,
        in_specs=placed,
        out_specs=(
            P(("expert", "hidden"), None),
            P("expert", None, "hidden"),
            P("expert", "hidden", None),
            P("expert", None),
            P("expert", None),
        ),
        check_vma=False,
    )
```

```python
import functools

import jax
import jax.numpy as jnp
from jax import lax
from jax.experimental import pallas as pl
from jax.experimental.pallas import tpu as pltpu
from jax.sharding import PartitionSpec as P

MESH = pl.DeviceIdType.MESH
F32 = jnp.float32
BF16 = jnp.bfloat16
N = 16
ROWS = 64
D = 2048
FD = 512
CH = 512
HALF = 32
VMEM_BYTES = 44 * 2**20


def dot_nn(a, b):
    return jnp.dot(a, b, preferred_element_type=F32)


def dot_nt(a, b):
    return lax.dot_general(a, b, (((1,), (1,)), ((), ())), preferred_element_type=F32)


def dot_tn(a, b):
    return lax.dot_general(a, b, (((0,), (0,)), ((), ())), preferred_element_type=F32)


def iota(shape, dim):
    return lax.broadcasted_iota(jnp.int32, shape, dim)


def onehot(mask):
    return jnp.where(mask, 1.0, 0.0).astype(BF16)


def chunk_pick(c, rows_first):
    shape = (ROWS, 256) if rows_first else (256, ROWS)
    k = iota(shape, 0 if rows_first else 1)
    q = iota(shape, 1 if rows_first else 0)
    return onehot(q == ((k >> 2) << 4) + 4 * c + (k & 3))


def gelu_pair(v):
    k0, k1 = 0.7978845608028654, 0.044715
    v2 = v * v
    t = jnp.tanh(k0 * (v + k1 * v2 * v))
    a = 0.5 * v * (1.0 + t)
    g = 0.5 * (1.0 + t) + 0.5 * v * (1.0 - t * t) * (k0 * (1.0 + 3.0 * k1 * v2))
    return a, g


def kernel(
    tok_h, cot_h, order_h, win_h, wout_h, gains_h, cent_h, pre_h, zout_h,
    gt_o, gwi_o, gwo_o, vec_o,
    tok, cot, order, gains, cent, win_t, wout_t, pre, pre_s, zout, act, slope, slope_s, dh, dh_s,
    a_dy, a_x, r_dy, r_x, dy, x, part, fa, fb, fc, fr1, fr2, stat, vec, dxs, rb, acc_i,
    load_sem, a2a_s, a2a_r, stat_s, stat_r, vec_s, vec_r, ret_s, ret_r, ag_s, ag_r, rs_s, rs_r, pair_s, pair_r,
):
    e = lax.axis_index("expert")
    h = lax.axis_index("hidden")
    xi = h // 4
    yc = h % 4
    yi = yc // 2
    ci = yc % 2
    yo = 1 - yi
    co = 1 - ci
    yoc = 2 * yo + ci
    xp, xm = (h + 4) % N, (h + 12) % N
    yn = h + 2 * (yo - yi)
    cn = h + co - ci

    barrier = pltpu.get_barrier_semaphore()

    sources = [(order_h, order), (cot_h, cot), (tok_h, tok), (wout_h.at[0], gwo_o), (win_h.at[0], gwi_o)]
    sources += [(pre_h.at[0, pl.ds(pl.multiple_of(((xi + k) % 4) * 256, 256), 256)], pre.at[k]) for k in range(4)]
    sources += [(cent_h, cent), (gains_h, gains), (zout_h.at[0], zout)]
    loads = [pltpu.make_async_copy(src, dst, load_sem.at[i]) for i, (src, dst) in enumerate(sources)]
    for c in loads[:2]:
        c.start()

    @pl.loop(1, N)
    def _(i):
        pl.semaphore_signal(barrier, 1, device_id={"expert": (e + i) % N, "hidden": h}, device_id_type=MESH)
        pl.semaphore_signal(barrier, 1, device_id={"expert": e, "hidden": (h + i) % N}, device_id_type=MESH)

    for c in loads[2:]:
        c.start()

    loads[0].wait()
    to_slot = onehot(iota((ROWS, ROWS), 0) == order[...])
    q = iota((256, ROWS), 0)
    spread = onehot(iota((256, ROWS), 1) == ((q >> 4) << 2) + (q & 3))
    pick = dot_nt(spread, to_slot)
    chunk_of = (q >> 2) & 3
    picks = [jnp.where(chunk_of == c, pick, 0.0).astype(BF16) for c in range(4)]

    def dispatch(src, dst):
        acc = dot_nn(picks[0], src[:, 0:CH])
        for c in range(1, 4):
            acc += dot_nn(picks[c], src[:, c * CH : (c + 1) * CH])
        dst[...] = acc.astype(BF16).reshape(N, 16, CH)

    def a2a_copy(src, dst, ssem, rsem, i):
        return pltpu.make_async_remote_copy(
            src_ref=src.at[(e + i) % N], dst_ref=dst.at[e], send_sem=ssem, recv_sem=rsem,
            device_id={"expert": (e + i) % N, "hidden": h}, device_id_type=MESH,
        )

    def a2a_start(t, src, dst):
        @pl.loop(1, N)
        def _(i):
            a2a_copy(src, dst, a2a_s.at[t, i], a2a_r.at[t, i], i).start()

        dst[e] = src[e]

    def a2a_arrived(t, src, dst):
        @pl.loop(1, N)
        def _(i):
            pltpu.make_async_remote_copy(
                src_ref=src.at[(e + i) % N], dst_ref=dst.at[(e + N - i) % N], send_sem=a2a_s.at[t, i], recv_sem=a2a_r.at[t, i],
                device_id={"expert": (e + i) % N, "hidden": h}, device_id_type=MESH,
            ).wait()

    loads[1].wait()
    dispatch(cot, a_dy)
    pl.semaphore_wait(barrier, 2 * (N - 1))
    a2a_start(0, a_dy, r_dy)
    loads[2].wait()
    dispatch(tok, a_x)
    a2a_start(1, a_x, r_x)

    lo, hi = pl.ds(0, HALF), pl.ds(HALF, HALF)

    def remote(sems, i, src, dst, where):
        return pltpu.make_async_remote_copy(
            src_ref=src, dst_ref=dst, send_sem=sems[0].at[i], recv_sem=sems[1].at[i],
            device_id={"expert": e, "hidden": where}, device_id_type=MESH,
        )

    pair_sems = (pair_s, pair_r)
    blocks = [(k, y) for k in range(4) for y in range(2)]

    def rows_of(y, c):
        return pl.ds(pl.multiple_of((2 * y + c) * ROWS, ROWS), ROWS)

    pair = [remote(pair_sems, i, pre.at[k, rows_of(y, co)], pre_s.at[k, y], cn) for i, (k, y) in enumerate(blocks)]
    pair.append(remote(pair_sems, 8, wout_t.at[0], wout_t.at[1], cn))
    pair.append(remote(pair_sems, 9, win_t.at[0], win_t.at[1], cn))
    loads[3].wait()
    wout_t[0] = gwo_o[...].T
    pair[8].start()
    for k in range(4):
        loads[5 + k].wait()
    for c in pair[:8]:
        c.start()
    loads[4].wait()
    win_t[0] = gwi_o[...].T
    pair[9].start()

    @pl.loop(0, 16)
    def _(i):
        k, rows = i // 4, pl.ds(pl.multiple_of((i % 4) * ROWS, ROWS), ROWS)
        a, g = gelu_pair(pre[k, rows].astype(F32))
        act[k, rows] = a.astype(BF16)
        slope[k, rows] = g

    def gather_plan(t, buf):
        sems = (ag_s.at[t], ag_r.at[t])
        plan = {}
        for part_of, r in (("lo", lo), ("hi", hi)):
            plan["own_xp_" + part_of] = (buf.at[0, yc, r], buf.at[3, yc, r], xp, buf.at[3, yc, r])
            plan["own_xm_" + part_of] = (buf.at[0, yc, r], buf.at[1, yc, r], xm, buf.at[1, yc, r])
            plan["own_y_" + part_of] = (buf.at[0, yc, r], buf.at[0, yc, r], yn, buf.at[0, yoc, r])
            plan["oy_xp_" + part_of] = (buf.at[0, yoc, r], buf.at[3, yoc, r], xp, buf.at[3, yoc, r])
            plan["oy_xm_" + part_of] = (buf.at[0, yoc, r], buf.at[1, yoc, r], xm, buf.at[1, yoc, r])
            plan["far_y_" + part_of] = (buf.at[2, yc, r], buf.at[2, yc, r], yn, buf.at[2, yoc, r])
        plan["half_xp"] = (buf.at[3, yc, lo], buf.at[2, yc, lo], xp, buf.at[2, yc, lo])
        plan["half_xm"] = (buf.at[1, yc, hi], buf.at[2, yc, hi], xm, buf.at[2, yc, hi])
        for k in range(4):
            plan["core_%d" % k] = (buf.at[k, yc], buf.at[k, yc], cn, buf.at[k, 2 * yi + co])
            plan["core_y%d" % k] = (buf.at[k, yoc], buf.at[k, yoc], cn, buf.at[k, 2 * yo + co])
        out = {}
        for i, (name, (src, dst, where, got)) in enumerate(plan.items()):
            out[name] = (remote(sems, i, src, dst, where), remote(sems, i, src, got, where))
        return out

    class Gather:
        def __init__(self, t, buf):
            self.plan = gather_plan(t, buf)

        def start(self, *names):
            for n in names:
                self.plan[n][0].start()

        def got(self, *names):
            for n in names:
                self.plan[n][1].wait_recv()

        def sent(self, *names):
            for n in names:
                self.plan[n][0].wait_send()

        def sent_all(self):
            self.sent(*self.plan)

    def collect(src, dst):
        rows = src[...].reshape(256, CH)
        for c in range(4):
            dst[0, yc, :, c * CH : (c + 1) * CH] = dot_nn(chunk_pick(c, True), rows).astype(BF16)

    gd = Gather(0, dy)
    gx = Gather(1, x)

    def first_hop_x(g):
        g.start("own_xp_lo", "own_xm_hi", "own_xp_hi", "own_xm_lo", "core_0")

    def first_hop_y(g):
        g.start("own_y_lo", "own_y_hi")

    def second_hop_a(g):
        g.got("own_xp_lo")
        g.start("half_xp")
        g.got("own_xm_hi")
        g.start("half_xm")

    def second_hop_b(g):
        g.got("own_y_lo")
        g.start("oy_xp_lo", "oy_xm_lo")
        g.got("own_y_hi")
        g.start("oy_xp_hi", "oy_xm_hi", "core_y0")

    def first_cores(g):
        g.got("own_xm_lo")
        g.start("core_1")
        g.got("own_xp_hi")
        g.start("core_3")

    def third_hop(g):
        g.got("half_xp")
        g.start("far_y_lo")
        g.got("half_xm")
        g.start("far_y_hi", "core_2")

    def last_hop(g):
        g.got("oy_xp_lo", "oy_xp_hi")
        g.start("core_y3")
        g.got("oy_xm_lo", "oy_xm_hi")
        g.start("core_y1")

    def last_far(g):
        g.got("far_y_lo", "far_y_hi")
        g.start("core_y2")

    rs_sems = (rs_s, rs_r)
    dh_copies = {}
    for k in range(4):
        for other, y in ((0, yi), (1, yo)):
            dh_copies[k, other] = remote(rs_sems, 2 * k + other, dh_s.at[k, y], dh.at[k, rows_of(y, ci)], cn)

    def forward(*shares):
        at = [(k, yo if other else yi) for k, other in shares]
        rows = [dy[k, 2 * y + ci] for k, y in at]
        rows = jnp.concatenate(rows, axis=0) if len(rows) > 1 else rows[0]
        mine, others = dot_nn(rows, wout_t[0]), dot_nn(rows, wout_t[1])
        left, right = [], []
        for i, (k, y) in enumerate(at):
            cut = slice(i * ROWS, (i + 1) * ROWS)
            left.append((mine[cut] * slope[k, rows_of(y, ci)]).astype(BF16))
            right.append((others[cut] * slope_s[k, y]).astype(BF16))
            dh[k, rows_of(y, ci)] = left[-1]
            dh_s[k, y] = right[-1]
        left = jnp.concatenate(left, axis=0) if len(at) > 1 else left[0]
        right = jnp.concatenate(right, axis=0) if len(at) > 1 else right[0]
        t = (dot_nn(left, win_t[0]) + dot_nn(right, win_t[1])).astype(BF16)
        for i, (k, y) in enumerate(at):
            part[k, y] = t[i * ROWS : (i + 1) * ROWS]
        for share in shares:
            dh_copies[share].start()

    def add(dst, *others):
        total = dst[...].astype(F32)
        for o in others:
            total += o[...].astype(F32)
        dst[...] = total.astype(BF16)

    rs = {
        "b_p": remote(rs_sems, 8, part.at[2, yi, lo], fb.at[0], xp),
        "b_m": remote(rs_sems, 9, part.at[2, yi, hi], fb.at[1], xm),
        "c_p": remote(rs_sems, 10, part.at[1, yi, lo], fc.at[0, lo], xp),
        "c_m": remote(rs_sems, 11, part.at[3, yi, hi], fc.at[1, hi], xm),
        "free_p": remote(rs_sems, 12, part.at[1, yi, hi], fc.at[0, hi], xp),
        "free_m": remote(rs_sems, 13, part.at[3, yi, lo], fc.at[1, lo], xm),
    }
    for i, (part_of, r) in enumerate((("lo", lo), ("hi", hi))):
        rs["a_p_" + part_of] = remote(rs_sems, 14 + 4 * i, part.at[1, yo, r], fa.at[0, r], xp)
        rs["a_m_" + part_of] = remote(rs_sems, 15 + 4 * i, part.at[3, yo, r], fa.at[1, r], xm)
        rs["r1_" + part_of] = remote(rs_sems, 16 + 4 * i, part.at[2, yo, r], fr1.at[r], yn)
        rs["r2_" + part_of] = remote(rs_sems, 17 + 4 * i, part.at[0, yo, r], fr2.at[r], yn)

    a2a_arrived(0, a_dy, r_dy)
    collect(r_dy, dy)
    first_hop_x(gd)
    first_hop_y(gd)
    for c in pair:
        c.wait_recv()

    @pl.loop(0, 8)
    def _(i):
        slope_s[i // 2, i % 2] = gelu_pair(pre_s[i // 2, i % 2].astype(F32))[1]

    second_hop_a(gd)
    second_hop_b(gd)
    a2a_arrived(1, a_x, r_x)
    collect(r_x, x)
    first_hop_x(gx)
    first_cores(gd)
    forward((1, 0), (3, 0), (0, 0), (0, 1))
    rs["free_p"].start()
    rs["free_m"].start()
    third_hop(gd)
    first_hop_y(gx)

    for c in loads[9:]:
        c.wait()
    xf = x[0, yc].astype(F32)
    dyf = dy[0, yc].astype(F32)
    r = lax.rsqrt(jnp.sum(xf * xf, axis=1, keepdims=True) * (1.0 / D) + 1e-06)
    s = jax.nn.sigmoid(jnp.sum(xf * cent[...], axis=1, keepdims=True))
    ds = jnp.sum(dyf * (xf + zout[...].astype(F32)), axis=1, keepdims=True)
    dlogit = ds * s * (1.0 - s)
    row_i, lane_i = iota((ROWS, 128), 0), iota((ROWS, 128), 1)
    s_mask, r_mask = lane_i == row_i, lane_i == row_i + ROWS
    stat[0, yc] = jnp.sum(jnp.where(s_mask, s, 0.0) + jnp.where(r_mask, r, 0.0), axis=0, keepdims=True)
    vec[h, 1] = jnp.sum(dlogit * xf, axis=0, keepdims=True)

    def stat_copy(i, got):
        to, frm = (h + i) % N, (h + N - i) % N
        slot = ((frm // 4 + 4 - xi) % 4, frm % 4) if got else ((xi + 4 - to // 4) % 4, yc)
        return pltpu.make_async_remote_copy(
            src_ref=stat.at[0, yc], dst_ref=stat.at[slot[0], slot[1]], send_sem=stat_s.at[i], recv_sem=stat_r.at[i],
            device_id={"expert": e, "hidden": to}, device_id_type=MESH,
        )

    @pl.loop(1, N)
    def _(i):
        stat_copy(i, False).start()

    forward((2, 0),)
    last_hop(gd)
    forward((1, 1), (3, 1))
    second_hop_a(gx)
    rs["a_p_lo"].start()
    rs["a_m_lo"].start()
    rs["a_p_hi"].start()
    rs["a_m_hi"].start()
    last_far(gd)
    forward((2, 1),)
    rs["r1_lo"].start()
    rs["r1_hi"].start()
    gd.got(*["core_%d" % k for k in range(4)], *["core_y%d" % k for k in range(4)])
    for c in dh_copies.values():
        c.wait_recv()

    @pl.loop(1, N)
    def _(i):
        stat_copy(i, True).wait()

    @pl.loop(0, 16)
    def _(i):
        k, j = i // 4, i % 4
        rows = pl.ds(pl.multiple_of(j * ROWS, ROWS), ROWS)
        line = stat[k, j]
        sj = jnp.sum(jnp.where(s_mask, line, 0.0), axis=1, keepdims=True)
        rj = jnp.sum(jnp.where(r_mask, line, 0.0), axis=1, keepdims=True)
        act[k, rows] = (act[k, rows].astype(F32) * sj).astype(BF16)
        dh[k, rows] = (dh[k, rows].astype(F32) * (sj * rj)).astype(BF16)

    def weight_out(n):
        cols = slice(n * 1024, (n + 1) * 1024)
        gwo_o[:, cols] = dot_tn(
            act[...].reshape(N * ROWS, FD), dy[:, :, :, cols].reshape(N * ROWS, 1024)
        ).astype(BF16)

    rs["r1_lo"].wait_recv()
    add(part.at[2, yi, lo], fr1.at[lo])
    rs["b_p"].start()
    rs["r1_hi"].wait_recv()
    add(part.at[2, yi, hi], fr1.at[hi])
    rs["b_m"].start()
    first_cores(gx)
    for part_of, half in (("lo", lo), ("hi", hi)):
        rs["a_p_" + part_of].wait_recv()
        rs["a_m_" + part_of].wait_recv()
        add(part.at[0, yo, half], fa.at[0, half], fa.at[1, half])
        rs["r2_" + part_of].start()
    rs["b_p"].wait_recv()
    add(part.at[1, yi, lo], fb.at[0])
    rs["c_p"].start()
    rs["b_m"].wait_recv()
    add(part.at[3, yi, hi], fb.at[1])
    rs["c_m"].start()
    second_hop_b(gx)
    third_hop(gx)
    weight_out(0)
    weight_out(1)

    gx.got("core_0", "core_1", "core_3", "core_y0")
    right = jnp.concatenate([dh[0], *(dh[k, pl.ds(pl.multiple_of(128 * yi, 128), 128)] for k in (1, 3))], axis=0)
    for n in range(8):
        cols = slice(n * 256, (n + 1) * 256)
        left = [x[0, :, :, cols].reshape(256, 256), *(x[k, pl.ds(2 * yi, 2), :, cols].reshape(128, 256) for k in (1, 3))]
        acc_i[cols] = dot_tn(jnp.concatenate(left, axis=0), right)

    for n in ("r2_lo", "r2_hi", "c_p", "c_m", "free_p", "free_m"):
        rs[n].wait_recv()
    dn = s * (
        part[0, yi].astype(F32) + fr2[...].astype(F32) + fc[0].astype(F32) + fc[1].astype(F32)
    )
    xf = x[0, yc].astype(F32)
    dyf = dy[0, yc].astype(F32)
    xhat = xf * r
    vec[h, 0] = jnp.sum(dn * xhat, axis=0, keepdims=True)
    qv = dn * gains[...]
    m = jnp.sum(qv * xhat, axis=1, keepdims=True) * (1.0 / D)
    dx = (dyf * (1.0 + s) + r * (qv - xhat * m) + dlogit * cent[...]).astype(BF16)
    acc = dot_nn(chunk_pick(0, False), dx[:, 0:CH])
    for c in range(1, 4):
        acc += dot_nn(chunk_pick(c, False), dx[:, c * CH : (c + 1) * CH])
    dxs[...] = acc.astype(BF16).reshape(N, 16, CH)

    def ret_copy(i, got):
        return pltpu.make_async_remote_copy(
            src_ref=dxs.at[(e + i) % N], dst_ref=rb.at[(e + N - i) % N if got else e],
            send_sem=ret_s.at[i], recv_sem=ret_r.at[i],
            device_id={"expert": (e + i) % N, "hidden": h}, device_id_type=MESH,
        )

    def vec_copy(i, got):
        return pltpu.make_async_remote_copy(
            src_ref=vec.at[h], dst_ref=vec.at[(h + N - i) % N if got else h], send_sem=vec_s.at[i], recv_sem=vec_r.at[i],
            device_id={"expert": e, "hidden": (h + i) % N}, device_id_type=MESH,
        )

    @pl.loop(1, N)
    def _(i):
        ret_copy(i, False).start()

    @pl.loop(1, N)
    def _(i):
        vec_copy(i, False).start()

    rb[e] = dxs[e]

    last_hop(gx)
    last_far(gx)
    gx.got("core_2", "core_y1", "core_y2", "core_y3")

    eye = iota((256, 256), 0) == iota((256, 256), 1)
    right = jnp.concatenate([dh[2], *(dh[k, pl.ds(pl.multiple_of(128 * yo, 128), 128)] for k in (1, 3))], axis=0)
    for n in range(8):
        cols = slice(n * 256, (n + 1) * 256)
        gain = jnp.sum(jnp.where(eye, gains[:, cols], 0.0), axis=1, keepdims=True)
        left = [x[2, :, :, cols].reshape(256, 256), *(x[k, pl.ds(2 * yo, 2), :, cols].reshape(128, 256) for k in (1, 3))]
        t = acc_i[cols] + dot_tn(jnp.concatenate(left, axis=0), right)
        gwi_o[cols] = (t * gain).astype(BF16)

    @pl.loop(1, N)
    def _(i):
        vec_copy(i, True).wait()

    total = vec[0]
    for i in range(1, N):
        total += vec[i]
    vec_o[...] = total

    @pl.loop(1, N)
    def _(i):
        ret_copy(i, True).wait()

    back = rb[...].reshape(256, CH)
    slot_of = dot_nt(to_slot, spread)
    q2 = iota((ROWS, 256), 1)
    for c in range(4):
        w = jnp.where(((q2 >> 2) & 3) == c, slot_of, 0.0).astype(BF16)
        gt_o[:, c * CH : (c + 1) * CH] = dot_nn(w, back).astype(BF16)

    gd.sent_all()
    gx.sent_all()
    for c in (*pair, *dh_copies.values(), *rs.values()):
        c.wait_send()


def write_out(gt, gwi, gwo, vec, gt_o, gwi_o, gwo_o, gg_o, gc_o, sem):
    pairs = ((gwi, gwi_o.at[0]), (gwo, gwo_o.at[0]), (gt, gt_o), (vec.at[0], gg_o), (vec.at[1], gc_o))
    copies = [pltpu.make_async_copy(a, b, sem.at[i]) for i, (a, b) in enumerate(pairs)]
    for c in copies:
        c.start()
    for c in copies:
        c.wait()


def shards(*args):
    vm = pl.BlockSpec(memory_space=pltpu.VMEM)
    hbm = pl.BlockSpec(memory_space=pltpu.HBM)
    anywhere = pl.BlockSpec(memory_space=pl.ANY)
    rows4 = (4, 4, ROWS, D)
    dma = pltpu.SemaphoreType.DMA
    args = [pltpu.with_memory_space_constraint(a, pltpu.HBM) for a in args]
    results = pl.pallas_call(
        kernel,
        out_shape=(
            pltpu.VMEM((ROWS, D), BF16),
            pltpu.VMEM((D, FD), BF16),
            pltpu.VMEM((FD, D), BF16),
            pltpu.VMEM((2, 1, D), F32),
        ),
        in_specs=[hbm] * 9,
        out_specs=(vm,) * 4,
        scratch_shapes=[
            pltpu.VMEM((ROWS, D), BF16),
            pltpu.VMEM((ROWS, D), BF16),
            pltpu.VMEM((1, ROWS), jnp.int32),
            pltpu.VMEM((1, D), F32),
            pltpu.VMEM((1, D), F32),
            pltpu.VMEM((2, FD, D), BF16),
            pltpu.VMEM((2, D, FD), BF16),
            pltpu.VMEM((4, 256, FD), BF16),
            pltpu.VMEM((4, 2, ROWS, FD), BF16),
            pltpu.VMEM((ROWS, D), BF16),
            pltpu.VMEM((4, 256, FD), BF16),
            pltpu.VMEM((4, 256, FD), F32),
            pltpu.VMEM((4, 2, ROWS, FD), F32),
            pltpu.VMEM((4, 256, FD), BF16),
            pltpu.VMEM((4, 2, ROWS, FD), BF16),
            pltpu.VMEM((N, 16, CH), BF16),
            pltpu.VMEM((N, 16, CH), BF16),
            pltpu.VMEM((N, 16, CH), BF16),
            pltpu.VMEM((N, 16, CH), BF16),
            pltpu.VMEM(rows4, BF16),
            pltpu.VMEM(rows4, BF16),
            pltpu.VMEM((4, 2, ROWS, D), BF16),
            pltpu.VMEM((2, ROWS, D), BF16),
            pltpu.VMEM((2, HALF, D), BF16),
            pltpu.VMEM((2, ROWS, D), BF16),
            pltpu.VMEM((ROWS, D), BF16),
            pltpu.VMEM((ROWS, D), BF16),
            pltpu.VMEM((4, 4, 1, 128), F32),
            pltpu.VMEM((N, 2, 1, D), F32),
            pltpu.VMEM((N, 16, CH), BF16),
            pltpu.VMEM((N, 16, CH), BF16),
            pltpu.VMEM((D, FD), F32),
            dma((12,)),
            dma((2, N)), dma((2, N)),
            dma((N,)), dma((N,)),
            dma((N,)), dma((N,)),
            dma((N,)), dma((N,)),
            dma((2, 22)), dma((2, 22)),
            dma((22,)), dma((22,)),
            dma((10,)), dma((10,)),
        ],
        compiler_params=pltpu.CompilerParams(
            collective_id=0, has_side_effects=True, vmem_limit_bytes=VMEM_BYTES
        ),
    )(*args)
    return pl.pallas_call(
        write_out,
        out_shape=(
            jax.ShapeDtypeStruct((ROWS, D), BF16),
            jax.ShapeDtypeStruct((1, D, FD), BF16),
            jax.ShapeDtypeStruct((1, FD, D), BF16),
            jax.ShapeDtypeStruct((1, D), F32),
            jax.ShapeDtypeStruct((1, D), F32),
        ),
        in_specs=[anywhere] * 4,
        out_specs=(hbm,) * 5,
        scratch_shapes=[dma((5,))],
        compiler_params=pltpu.CompilerParams(vmem_limit_bytes=2**20),
    )(*results)


def solution(mesh):
    placed = (
        P(("expert", "hidden"), None),
        P(("expert", "hidden"), None),
        P(("expert", "hidden"), None),
        P("expert", None, "hidden"),
        P("expert", "hidden", None),
        P("expert", None),
        P("expert", None),
        P("expert", None, "hidden"),
        P("expert", "hidden", None),
    )
    return jax.shard_map(
        shards,
        mesh=mesh,
        in_specs=placed,
        out_specs=(
            P(("expert", "hidden"), None),
            P("expert", None, "hidden"),
            P("expert", "hidden", None),
            P("expert", None),
            P("expert", None),
        ),
        check_vma=False,
    )
```

```python
import functools

import jax
import jax.numpy as jnp
from jax import lax
from jax.experimental import pallas as pl
from jax.experimental.pallas import tpu as pltpu
from jax.sharding import PartitionSpec as P

MESH = pl.DeviceIdType.MESH
F32 = jnp.float32
BF16 = jnp.bfloat16
N = 16
ROWS = 64
D = 2048
FD = 512
CH = 512
HALF = 32
VMEM_BYTES = 44 * 2**20


def dot_nn(a, b):
    return jnp.dot(a, b, preferred_element_type=F32)


def dot_nt(a, b):
    return lax.dot_general(a, b, (((1,), (1,)), ((), ())), preferred_element_type=F32)


def dot_tn(a, b):
    return lax.dot_general(a, b, (((0,), (0,)), ((), ())), preferred_element_type=F32)


def iota(shape, dim):
    return lax.broadcasted_iota(jnp.int32, shape, dim)


def onehot(mask):
    return jnp.where(mask, 1.0, 0.0).astype(BF16)


def chunk_pick(c, rows_first):
    shape = (ROWS, 256) if rows_first else (256, ROWS)
    k = iota(shape, 0 if rows_first else 1)
    q = iota(shape, 1 if rows_first else 0)
    return onehot(q == ((k >> 2) << 4) + 4 * c + (k & 3))


def gelu_pair(v):
    k0, k1 = 0.7978845608028654, 0.044715
    v2 = v * v
    t = jnp.tanh(k0 * (v + k1 * v2 * v))
    a = 0.5 * v * (1.0 + t)
    g = 0.5 * (1.0 + t) + 0.5 * v * (1.0 - t * t) * (k0 * (1.0 + 3.0 * k1 * v2))
    return a, g


def kernel(
    tok_h, cot_h, order_h, win_h, wout_h, gains_h, cent_h, pre_h, zout_h,
    gt_o, gwi_o, gwo_o, vec_o,
    tok, cot, order, gains, cent, win_t, wout_t, pre, pre_s, zout, act, slope, slope_s, dh, dh_s,
    a_dy, a_x, r_dy, r_x, dy, x, part, fa, fb, fc, fr1, fr2, stat, vec, dxs, rb, acc_i,
    load_sem, a2a_s, a2a_r, stat_s, stat_r, vec_s, vec_r, ret_s, ret_r, ag_s, ag_r, rs_s, rs_r, pair_s, pair_r,
):
    e = lax.axis_index("expert")
    h = lax.axis_index("hidden")
    xi = h // 4
    yc = h % 4
    yi = yc // 2
    ci = yc % 2
    yo = 1 - yi
    co = 1 - ci
    yoc = 2 * yo + ci
    xp, xm = (h + 4) % N, (h + 12) % N
    yn = h + 2 * (yo - yi)
    cn = h + co - ci

    barrier = pltpu.get_barrier_semaphore()

    sources = [(order_h, order), (cot_h, cot), (tok_h, tok), (wout_h.at[0], gwo_o), (win_h.at[0], gwi_o)]
    sources += [(pre_h.at[0, pl.ds(pl.multiple_of(((xi + k) % 4) * 256, 256), 256)], pre.at[k]) for k in range(4)]
    sources += [(cent_h, cent), (gains_h, gains), (zout_h.at[0], zout)]
    loads = [pltpu.make_async_copy(src, dst, load_sem.at[i]) for i, (src, dst) in enumerate(sources)]
    for c in loads[:2]:
        c.start()

    for i in range(1, N):
        pl.semaphore_signal(barrier, 1, device_id={"expert": (e + i) % N, "hidden": h}, device_id_type=MESH)
        pl.semaphore_signal(barrier, 1, device_id={"expert": e, "hidden": (h + i) % N}, device_id_type=MESH)

    for c in loads[2:]:
        c.start()

    loads[0].wait()
    to_slot = onehot(iota((ROWS, ROWS), 0) == order[...])
    q = iota((256, ROWS), 0)
    spread = onehot(iota((256, ROWS), 1) == ((q >> 4) << 2) + (q & 3))
    pick = dot_nt(spread, to_slot)
    chunk_of = (q >> 2) & 3
    picks = [jnp.where(chunk_of == c, pick, 0.0).astype(BF16) for c in range(4)]

    def dispatch(src, dst):
        acc = dot_nn(picks[0], src[:, 0:CH])
        for c in range(1, 4):
            acc += dot_nn(picks[c], src[:, c * CH : (c + 1) * CH])
        dst[...] = acc.astype(BF16).reshape(N, 16, CH)

    def a2a_copy(src, dst, ssem, rsem, i):
        return pltpu.make_async_remote_copy(
            src_ref=src.at[(e + i) % N], dst_ref=dst.at[e], send_sem=ssem, recv_sem=rsem,
            device_id={"expert": (e + i) % N, "hidden": h}, device_id_type=MESH,
        )

    def a2a_start(t, src, dst):
        @pl.loop(1, N)
        def _(i):
            a2a_copy(src, dst, a2a_s.at[t, i], a2a_r.at[t, i], i).start()

        dst[e] = src[e]

    def a2a_arrived(t, src, dst):
        @pl.loop(1, N)
        def _(i):
            pltpu.make_async_remote_copy(
                src_ref=src.at[(e + i) % N], dst_ref=dst.at[(e + N - i) % N], send_sem=a2a_s.at[t, i], recv_sem=a2a_r.at[t, i],
                device_id={"expert": (e + i) % N, "hidden": h}, device_id_type=MESH,
            ).wait()

    loads[1].wait()
    dispatch(cot, a_dy)
    pl.semaphore_wait(barrier, 2 * (N - 1))
    a2a_start(0, a_dy, r_dy)
    loads[2].wait()
    dispatch(tok, a_x)
    a2a_start(1, a_x, r_x)

    lo, hi = pl.ds(0, HALF), pl.ds(HALF, HALF)

    def remote(sems, i, src, dst, where):
        return pltpu.make_async_remote_copy(
            src_ref=src, dst_ref=dst, send_sem=sems[0].at[i], recv_sem=sems[1].at[i],
            device_id={"expert": e, "hidden": where}, device_id_type=MESH,
        )

    pair_sems = (pair_s, pair_r)
    blocks = [(k, y) for k in range(4) for y in range(2)]

    def rows_of(y, c):
        return pl.ds(pl.multiple_of((2 * y + c) * ROWS, ROWS), ROWS)

    pair = [remote(pair_sems, i, pre.at[k, rows_of(y, co)], pre_s.at[k, y], cn) for i, (k, y) in enumerate(blocks)]
    pair.append(remote(pair_sems, 8, wout_t.at[0], wout_t.at[1], cn))
    pair.append(remote(pair_sems, 9, win_t.at[0], win_t.at[1], cn))
    loads[3].wait()
    wout_t[0] = gwo_o[...].T
    pair[8].start()
    for k in range(4):
        loads[5 + k].wait()
    for c in pair[:8]:
        c.start()
    loads[4].wait()
    win_t[0] = gwi_o[...].T
    pair[9].start()

    @pl.loop(0, 16)
    def _(i):
        k, rows = i // 4, pl.ds(pl.multiple_of((i % 4) * ROWS, ROWS), ROWS)
        a, g = gelu_pair(pre[k, rows].astype(F32))
        act[k, rows] = a.astype(BF16)
        slope[k, rows] = g

    def gather_plan(t, buf):
        sems = (ag_s.at[t], ag_r.at[t])
        plan = {}
        for part_of, r in (("lo", lo), ("hi", hi)):
            plan["own_xp_" + part_of] = (buf.at[0, yc, r], buf.at[3, yc, r], xp, buf.at[3, yc, r])
            plan["own_xm_" + part_of] = (buf.at[0, yc, r], buf.at[1, yc, r], xm, buf.at[1, yc, r])
            plan["own_y_" + part_of] = (buf.at[0, yc, r], buf.at[0, yc, r], yn, buf.at[0, yoc, r])
            plan["oy_xp_" + part_of] = (buf.at[0, yoc, r], buf.at[3, yoc, r], xp, buf.at[3, yoc, r])
            plan["oy_xm_" + part_of] = (buf.at[0, yoc, r], buf.at[1, yoc, r], xm, buf.at[1, yoc, r])
            plan["far_y_" + part_of] = (buf.at[2, yc, r], buf.at[2, yc, r], yn, buf.at[2, yoc, r])
        plan["half_xp"] = (buf.at[3, yc, lo], buf.at[2, yc, lo], xp, buf.at[2, yc, lo])
        plan["half_xm"] = (buf.at[1, yc, hi], buf.at[2, yc, hi], xm, buf.at[2, yc, hi])
        for k in range(4):
            plan["core_%d" % k] = (buf.at[k, yc], buf.at[k, yc], cn, buf.at[k, 2 * yi + co])
            plan["core_y%d" % k] = (buf.at[k, yoc], buf.at[k, yoc], cn, buf.at[k, 2 * yo + co])
        out = {}
        for i, (name, (src, dst, where, got)) in enumerate(plan.items()):
            out[name] = (remote(sems, i, src, dst, where), remote(sems, i, src, got, where))
        return out

    class Gather:
        def __init__(self, t, buf):
            self.plan = gather_plan(t, buf)

        def start(self, *names):
            for n in names:
                self.plan[n][0].start()

        def got(self, *names):
            for n in names:
                self.plan[n][1].wait_recv()

        def sent(self, *names):
            for n in names:
                self.plan[n][0].wait_send()

        def sent_all(self):
            self.sent(*self.plan)

    def collect(src, dst):
        rows = src[...].reshape(256, CH)
        for c in range(4):
            dst[0, yc, :, c * CH : (c + 1) * CH] = dot_nn(chunk_pick(c, True), rows).astype(BF16)

    gd = Gather(0, dy)
    gx = Gather(1, x)

    def first_hop_x(g):
        g.start("own_xp_lo", "own_xm_hi", "own_xp_hi", "own_xm_lo", "core_0")

    def first_hop_y(g):
        g.start("own_y_lo", "own_y_hi")

    def second_hop_a(g):
        g.got("own_xp_lo")
        g.start("half_xp")
        g.got("own_xm_hi")
        g.start("half_xm")

    def second_hop_b(g):
        g.got("own_y_lo")
        g.start("oy_xp_lo", "oy_xm_lo")
        g.got("own_y_hi")
        g.start("oy_xp_hi", "oy_xm_hi", "core_y0")

    def first_cores(g):
        g.got("own_xm_lo")
        g.start("core_1")
        g.got("own_xp_hi")
        g.start("core_3")

    def third_hop(g):
        g.got("half_xp")
        g.start("far_y_lo")
        g.got("half_xm")
        g.start("far_y_hi", "core_2")

    def last_hop(g):
        g.got("oy_xp_lo", "oy_xp_hi")
        g.start("core_y3")
        g.got("oy_xm_lo", "oy_xm_hi")
        g.start("core_y1")

    def last_far(g):
        g.got("far_y_lo", "far_y_hi")
        g.start("core_y2")

    rs_sems = (rs_s, rs_r)
    dh_copies = {}
    for k in range(4):
        for other, y in ((0, yi), (1, yo)):
            dh_copies[k, other] = remote(rs_sems, 2 * k + other, dh_s.at[k, y], dh.at[k, rows_of(y, ci)], cn)

    def forward(*shares):
        at = [(k, yo if other else yi) for k, other in shares]
        rows = [dy[k, 2 * y + ci] for k, y in at]
        rows = jnp.concatenate(rows, axis=0) if len(rows) > 1 else rows[0]
        mine, others = dot_nn(rows, wout_t[0]), dot_nn(rows, wout_t[1])
        left, right = [], []
        for i, (k, y) in enumerate(at):
            cut = slice(i * ROWS, (i + 1) * ROWS)
            left.append((mine[cut] * slope[k, rows_of(y, ci)]).astype(BF16))
            right.append((others[cut] * slope_s[k, y]).astype(BF16))
            dh[k, rows_of(y, ci)] = left[-1]
            dh_s[k, y] = right[-1]
        left = jnp.concatenate(left, axis=0) if len(at) > 1 else left[0]
        right = jnp.concatenate(right, axis=0) if len(at) > 1 else right[0]
        t = (dot_nn(left, win_t[0]) + dot_nn(right, win_t[1])).astype(BF16)
        for i, (k, y) in enumerate(at):
            part[k, y] = t[i * ROWS : (i + 1) * ROWS]
        for share in shares:
            dh_copies[share].start()

    def add(dst, *others):
        total = dst[...].astype(F32)
        for o in others:
            total += o[...].astype(F32)
        dst[...] = total.astype(BF16)

    rs = {
        "b_p": remote(rs_sems, 8, part.at[2, yi, lo], fb.at[0], xp),
        "b_m": remote(rs_sems, 9, part.at[2, yi, hi], fb.at[1], xm),
        "c_p": remote(rs_sems, 10, part.at[1, yi, lo], fc.at[0, lo], xp),
        "c_m": remote(rs_sems, 11, part.at[3, yi, hi], fc.at[1, hi], xm),
        "free_p": remote(rs_sems, 12, part.at[1, yi, hi], fc.at[0, hi], xp),
        "free_m": remote(rs_sems, 13, part.at[3, yi, lo], fc.at[1, lo], xm),
    }
    for i, (part_of, r) in enumerate((("lo", lo), ("hi", hi))):
        rs["a_p_" + part_of] = remote(rs_sems, 14 + 4 * i, part.at[1, yo, r], fa.at[0, r], xp)
        rs["a_m_" + part_of] = remote(rs_sems, 15 + 4 * i, part.at[3, yo, r], fa.at[1, r], xm)
        rs["r1_" + part_of] = remote(rs_sems, 16 + 4 * i, part.at[2, yo, r], fr1.at[r], yn)
        rs["r2_" + part_of] = remote(rs_sems, 17 + 4 * i, part.at[0, yo, r], fr2.at[r], yn)

    a2a_arrived(0, a_dy, r_dy)
    collect(r_dy, dy)
    first_hop_x(gd)
    first_hop_y(gd)
    for c in pair:
        c.wait_recv()

    @pl.loop(0, 8)
    def _(i):
        slope_s[i // 2, i % 2] = gelu_pair(pre_s[i // 2, i % 2].astype(F32))[1]

    second_hop_a(gd)
    second_hop_b(gd)
    a2a_arrived(1, a_x, r_x)
    collect(r_x, x)
    first_hop_x(gx)
    first_cores(gd)
    forward((1, 0), (3, 0), (0, 0), (0, 1))
    rs["free_p"].start()
    rs["free_m"].start()
    third_hop(gd)
    first_hop_y(gx)

    for c in loads[9:]:
        c.wait()
    xf = x[0, yc].astype(F32)
    dyf = dy[0, yc].astype(F32)
    r = lax.rsqrt(jnp.sum(xf * xf, axis=1, keepdims=True) * (1.0 / D) + 1e-06)
    s = jax.nn.sigmoid(jnp.sum(xf * cent[...], axis=1, keepdims=True))
    ds = jnp.sum(dyf * (xf + zout[...].astype(F32)), axis=1, keepdims=True)
    dlogit = ds * s * (1.0 - s)
    row_i, lane_i = iota((ROWS, 128), 0), iota((ROWS, 128), 1)
    s_mask, r_mask = lane_i == row_i, lane_i == row_i + ROWS
    stat[0, yc] = jnp.sum(jnp.where(s_mask, s, 0.0) + jnp.where(r_mask, r, 0.0), axis=0, keepdims=True)
    vec[h, 1] = jnp.sum(dlogit * xf, axis=0, keepdims=True)

    def stat_copy(i, got):
        to, frm = (h + i) % N, (h + N - i) % N
        slot = ((frm // 4 + 4 - xi) % 4, frm % 4) if got else ((xi + 4 - to // 4) % 4, yc)
        return pltpu.make_async_remote_copy(
            src_ref=stat.at[0, yc], dst_ref=stat.at[slot[0], slot[1]], send_sem=stat_s.at[i], recv_sem=stat_r.at[i],
            device_id={"expert": e, "hidden": to}, device_id_type=MESH,
        )

    @pl.loop(1, N)
    def _(i):
        stat_copy(i, False).start()

    forward((2, 0),)
    last_hop(gd)
    forward((1, 1), (3, 1))
    second_hop_a(gx)
    rs["a_p_lo"].start()
    rs["a_m_lo"].start()
    rs["a_p_hi"].start()
    rs["a_m_hi"].start()
    last_far(gd)
    forward((2, 1),)
    rs["r1_lo"].start()
    rs["r1_hi"].start()
    gd.got(*["core_%d" % k for k in range(4)], *["core_y%d" % k for k in range(4)])
    for c in dh_copies.values():
        c.wait_recv()

    @pl.loop(1, N)
    def _(i):
        stat_copy(i, True).wait()

    @pl.loop(0, 16)
    def _(i):
        k, j = i // 4, i % 4
        rows = pl.ds(pl.multiple_of(j * ROWS, ROWS), ROWS)
        line = stat[k, j]
        sj = jnp.sum(jnp.where(s_mask, line, 0.0), axis=1, keepdims=True)
        rj = jnp.sum(jnp.where(r_mask, line, 0.0), axis=1, keepdims=True)
        act[k, rows] = (act[k, rows].astype(F32) * sj).astype(BF16)
        dh[k, rows] = (dh[k, rows].astype(F32) * (sj * rj)).astype(BF16)

    def weight_out(n):
        cols = slice(n * 1024, (n + 1) * 1024)
        gwo_o[:, cols] = dot_tn(
            act[...].reshape(N * ROWS, FD), dy[:, :, :, cols].reshape(N * ROWS, 1024)
        ).astype(BF16)

    rs["r1_lo"].wait_recv()
    add(part.at[2, yi, lo], fr1.at[lo])
    rs["b_p"].start()
    rs["r1_hi"].wait_recv()
    add(part.at[2, yi, hi], fr1.at[hi])
    rs["b_m"].start()
    first_cores(gx)
    for part_of, half in (("lo", lo), ("hi", hi)):
        rs["a_p_" + part_of].wait_recv()
        rs["a_m_" + part_of].wait_recv()
        add(part.at[0, yo, half], fa.at[0, half], fa.at[1, half])
        rs["r2_" + part_of].start()
    rs["b_p"].wait_recv()
    add(part.at[1, yi, lo], fb.at[0])
    rs["c_p"].start()
    rs["b_m"].wait_recv()
    add(part.at[3, yi, hi], fb.at[1])
    rs["c_m"].start()
    second_hop_b(gx)
    third_hop(gx)
    weight_out(0)
    weight_out(1)

    gx.got("core_0", "core_1", "core_3", "core_y0")
    right = jnp.concatenate([dh[0], *(dh[k, pl.ds(pl.multiple_of(128 * yi, 128), 128)] for k in (1, 3))], axis=0)
    for n in range(8):
        cols = slice(n * 256, (n + 1) * 256)
        left = [x[0, :, :, cols].reshape(256, 256), *(x[k, pl.ds(2 * yi, 2), :, cols].reshape(128, 256) for k in (1, 3))]
        acc_i[cols] = dot_tn(jnp.concatenate(left, axis=0), right)

    for n in ("r2_lo", "r2_hi", "c_p", "c_m", "free_p", "free_m"):
        rs[n].wait_recv()
    dn = s * (
        part[0, yi].astype(F32) + fr2[...].astype(F32) + fc[0].astype(F32) + fc[1].astype(F32)
    )
    xf = x[0, yc].astype(F32)
    dyf = dy[0, yc].astype(F32)
    xhat = xf * r
    vec[h, 0] = jnp.sum(dn * xhat, axis=0, keepdims=True)
    qv = dn * gains[...]
    m = jnp.sum(qv * xhat, axis=1, keepdims=True) * (1.0 / D)
    dx = (dyf * (1.0 + s) + r * (qv - xhat * m) + dlogit * cent[...]).astype(BF16)
    acc = dot_nn(chunk_pick(0, False), dx[:, 0:CH])
    for c in range(1, 4):
        acc += dot_nn(chunk_pick(c, False), dx[:, c * CH : (c + 1) * CH])
    dxs[...] = acc.astype(BF16).reshape(N, 16, CH)

    def ret_copy(i, got):
        return pltpu.make_async_remote_copy(
            src_ref=dxs.at[(e + i) % N], dst_ref=rb.at[(e + N - i) % N if got else e],
            send_sem=ret_s.at[i], recv_sem=ret_r.at[i],
            device_id={"expert": (e + i) % N, "hidden": h}, device_id_type=MESH,
        )

    def vec_copy(i, got):
        return pltpu.make_async_remote_copy(
            src_ref=vec.at[h], dst_ref=vec.at[(h + N - i) % N if got else h], send_sem=vec_s.at[i], recv_sem=vec_r.at[i],
            device_id={"expert": e, "hidden": (h + i) % N}, device_id_type=MESH,
        )

    @pl.loop(1, N)
    def _(i):
        ret_copy(i, False).start()

    @pl.loop(1, N)
    def _(i):
        vec_copy(i, False).start()

    rb[e] = dxs[e]

    last_hop(gx)
    last_far(gx)
    gx.got("core_2", "core_y1", "core_y2", "core_y3")

    eye = iota((256, 256), 0) == iota((256, 256), 1)
    right = jnp.concatenate([dh[2], *(dh[k, pl.ds(pl.multiple_of(128 * yo, 128), 128)] for k in (1, 3))], axis=0)
    for n in range(8):
        cols = slice(n * 256, (n + 1) * 256)
        gain = jnp.sum(jnp.where(eye, gains[:, cols], 0.0), axis=1, keepdims=True)
        left = [x[2, :, :, cols].reshape(256, 256), *(x[k, pl.ds(2 * yo, 2), :, cols].reshape(128, 256) for k in (1, 3))]
        t = acc_i[cols] + dot_tn(jnp.concatenate(left, axis=0), right)
        gwi_o[cols] = (t * gain).astype(BF16)

    @pl.loop(1, N)
    def _(i):
        vec_copy(i, True).wait()

    total = vec[0]
    for i in range(1, N):
        total += vec[i]
    vec_o[...] = total

    @pl.loop(1, N)
    def _(i):
        ret_copy(i, True).wait()

    back = rb[...].reshape(256, CH)
    slot_of = dot_nt(to_slot, spread)
    q2 = iota((ROWS, 256), 1)
    for c in range(4):
        w = jnp.where(((q2 >> 2) & 3) == c, slot_of, 0.0).astype(BF16)
        gt_o[:, c * CH : (c + 1) * CH] = dot_nn(w, back).astype(BF16)

    gd.sent_all()
    gx.sent_all()
    for c in (*pair, *dh_copies.values(), *rs.values()):
        c.wait_send()


def write_out(gt, gwi, gwo, vec, gt_o, gwi_o, gwo_o, gg_o, gc_o, sem):
    pairs = ((gwi, gwi_o.at[0]), (gwo, gwo_o.at[0]), (gt, gt_o), (vec.at[0], gg_o), (vec.at[1], gc_o))
    copies = [pltpu.make_async_copy(a, b, sem.at[i]) for i, (a, b) in enumerate(pairs)]
    for c in copies:
        c.start()
    for c in copies:
        c.wait()


def shards(*args):
    vm = pl.BlockSpec(memory_space=pltpu.VMEM)
    hbm = pl.BlockSpec(memory_space=pltpu.HBM)
    anywhere = pl.BlockSpec(memory_space=pl.ANY)
    rows4 = (4, 4, ROWS, D)
    dma = pltpu.SemaphoreType.DMA
    args = [pltpu.with_memory_space_constraint(a, pltpu.HBM) for a in args]
    results = pl.pallas_call(
        kernel,
        out_shape=(
            pltpu.VMEM((ROWS, D), BF16),
            pltpu.VMEM((D, FD), BF16),
            pltpu.VMEM((FD, D), BF16),
            pltpu.VMEM((2, 1, D), F32),
        ),
        in_specs=[hbm] * 9,
        out_specs=(vm,) * 4,
        scratch_shapes=[
            pltpu.VMEM((ROWS, D), BF16),
            pltpu.VMEM((ROWS, D), BF16),
            pltpu.VMEM((1, ROWS), jnp.int32),
            pltpu.VMEM((1, D), F32),
            pltpu.VMEM((1, D), F32),
            pltpu.VMEM((2, FD, D), BF16),
            pltpu.VMEM((2, D, FD), BF16),
            pltpu.VMEM((4, 256, FD), BF16),
            pltpu.VMEM((4, 2, ROWS, FD), BF16),
            pltpu.VMEM((ROWS, D), BF16),
            pltpu.VMEM((4, 256, FD), BF16),
            pltpu.VMEM((4, 256, FD), F32),
            pltpu.VMEM((4, 2, ROWS, FD), F32),
            pltpu.VMEM((4, 256, FD), BF16),
            pltpu.VMEM((4, 2, ROWS, FD), BF16),
            pltpu.VMEM((N, 16, CH), BF16),
            pltpu.VMEM((N, 16, CH), BF16),
            pltpu.VMEM((N, 16, CH), BF16),
            pltpu.VMEM((N, 16, CH), BF16),
            pltpu.VMEM(rows4, BF16),
            pltpu.VMEM(rows4, BF16),
            pltpu.VMEM((4, 2, ROWS, D), BF16),
            pltpu.VMEM((2, ROWS, D), BF16),
            pltpu.VMEM((2, HALF, D), BF16),
            pltpu.VMEM((2, ROWS, D), BF16),
            pltpu.VMEM((ROWS, D), BF16),
            pltpu.VMEM((ROWS, D), BF16),
            pltpu.VMEM((4, 4, 1, 128), F32),
            pltpu.VMEM((N, 2, 1, D), F32),
            pltpu.VMEM((N, 16, CH), BF16),
            pltpu.VMEM((N, 16, CH), BF16),
            pltpu.VMEM((D, FD), F32),
            dma((12,)),
            dma((2, N)), dma((2, N)),
            dma((N,)), dma((N,)),
            dma((N,)), dma((N,)),
            dma((N,)), dma((N,)),
            dma((2, 22)), dma((2, 22)),
            dma((22,)), dma((22,)),
            dma((10,)), dma((10,)),
        ],
        compiler_params=pltpu.CompilerParams(
            collective_id=0, has_side_effects=True, vmem_limit_bytes=VMEM_BYTES
        ),
    )(*args)
    return pl.pallas_call(
        write_out,
        out_shape=(
            jax.ShapeDtypeStruct((ROWS, D), BF16),
            jax.ShapeDtypeStruct((1, D, FD), BF16),
            jax.ShapeDtypeStruct((1, FD, D), BF16),
            jax.ShapeDtypeStruct((1, D), F32),
            jax.ShapeDtypeStruct((1, D), F32),
        ),
        in_specs=[anywhere] * 4,
        out_specs=(hbm,) * 5,
        scratch_shapes=[dma((5,))],
        compiler_params=pltpu.CompilerParams(vmem_limit_bytes=2**20),
    )(*results)


def solution(mesh):
    placed = (
        P(("expert", "hidden"), None),
        P(("expert", "hidden"), None),
        P(("expert", "hidden"), None),
        P("expert", None, "hidden"),
        P("expert", "hidden", None),
        P("expert", None),
        P("expert", None),
        P("expert", None, "hidden"),
        P("expert", "hidden", None),
    )
    return jax.shard_map(
        shards,
        mesh=mesh,
        in_specs=placed,
        out_specs=(
            P(("expert", "hidden"), None),
            P("expert", None, "hidden"),
            P("expert", "hidden", None),
            P("expert", None),
            P("expert", None),
        ),
        check_vma=False,
    )
```
